32 devices in a mesh: seq: 4 (over y, x), res: 8 (over z, core).
Axes of the slice: x: 2, y: 2, z: 4, core: 2. Of those that a mesh axis runs over, the one named last changes fastest.
Arguments:
- alignment_tensor: float32 [192, 128, 256], P('seq', 'res'), may hold values from -24 to 24
- standardizer_factors: float32 [3, 256], replicated, may hold values from 0.25 to 1.75
- standardizer_offsets: float32 [3, 256], replicated, may hold values from -3 to 3
- horizontal_entry_matrix: bfloat16 [256, 1024], replicated, may hold values from -4 to 4
- horizontal_sigmoid_offset: float32 [256], replicated, may hold values from -4 to 4
- horizontal_exit_matrix: bfloat16 [256, 256], replicated, may hold values from -1 to 1
- horizontal_exit_offset: float32 [256], replicated, may hold values from -2 to 2
- vertical_entry_matrix: bfloat16 [256, 1024], replicated, may hold values from -4 to 4
- vertical_sigmoid_offset: float32 [256], replicated, may hold values from -4 to 4
- vertical_exit_matrix: bfloat16 [256, 256], replicated, may hold values from -1 to 1
- vertical_exit_offset: float32 [256], replicated, may hold values from -2 to 2
- feedforward_first_matrix: bfloat16 [256, 1024], replicated, may hold values from -0.375 to 0.375
- feedforward_first_offset: float32 [1024], replicated, may hold values from -3 to 3
- feedforward_second_matrix: bfloat16 [1024, 256], replicated, may hold values from -0.25 to 0.25
- feedforward_second_offset: float32 [256], replicated, may hold values from -2 to 2
Outputs:
- updated_msa: float32 [192, 128, 256], P('seq', 'res')
The draws below stay inside these ranges and needn't reach their ends.
All inputs are finite; a program needn't handle non-finite values.
Results may differ from the reference program's by a relative error of at most 0.012.
Values may be sent and summed in bfloat16 or wider, within the bound.
A program may use at most 64 MiB of HBM per device.

```python
import jax
import jax.numpy as jnp
from jax import lax

C = 256
HEADS = 8
FF = 1024
SEQS = 192
RESIDUES = 128


def draw_alignment_tensor(key, part):
    own_key = jax.random.fold_in(key, 13)
    base = jax.random.normal(jax.random.fold_in(own_key, 1), (SEQS, RESIDUES, C), jnp.float32)
    return jnp.clip(base, -24.0, 24.0)


def projection_draw(key, salt):
    own_key = jax.random.fold_in(key, salt)
    columns = jnp.arange(4 * C)
    column_scale = jnp.where(columns < 2 * C, 1.4, 1.0)
    base = jax.random.normal(own_key, (C, 4 * C), jnp.float32) * column_scale / jnp.sqrt(jnp.float32(C))
    return jnp.clip(base, -4.0, 4.0)


def draw_horizontal_entry_matrix(key, part):
    return projection_draw(key, 21).astype(jnp.bfloat16)


def draw_vertical_entry_matrix(key, part):
    return projection_draw(key, 22).astype(jnp.bfloat16)


def gaussian(key, dims, scale, most, dtype=jnp.bfloat16):
    values = jax.random.normal(key, dims, jnp.float32) * scale
    return jnp.minimum(jnp.maximum(values, -most), most).astype(dtype)


def setup_inputs(seed: int = 0) -> dict:
    keys = jax.random.split(jax.random.key(seed), 16)
    alignment_tensor = draw_alignment_tensor(jax.random.fold_in(keys[15], 71), 0)
    standardizer_factors = jnp.clip(1.0 + 0.15 * jax.random.normal(keys[1], (3, C), jnp.float32), 0.25, 1.75)
    standardizer_offsets = gaussian(keys[2], (3, C), 0.5, 3.0, jnp.float32)
    horizontal_entry_matrix = draw_horizontal_entry_matrix(jax.random.fold_in(keys[15], 71), 0)
    horizontal_sigmoid_offset = gaussian(keys[4], (C,), 1.0, 4.0, jnp.float32)
    horizontal_exit_matrix = gaussian(keys[5], (C, C), (C // 8) ** -0.5, 1.0)
    horizontal_exit_offset = gaussian(keys[6], (C,), 0.3, 2.0, jnp.float32)
    vertical_entry_matrix = draw_vertical_entry_matrix(jax.random.fold_in(keys[15], 71), 0)
    vertical_sigmoid_offset = gaussian(keys[8], (C,), 1.0, 4.0, jnp.float32)
    vertical_exit_matrix = gaussian(keys[9], (C, C), (C // 8) ** -0.5, 1.0)
    vertical_exit_offset = gaussian(keys[10], (C,), 0.3, 2.0, jnp.float32)
    feedforward_first_matrix = gaussian(keys[11], (C, FF), C ** -0.5, 0.375)
    feedforward_first_offset = gaussian(keys[12], (FF,), 0.5, 3.0, jnp.float32)
    feedforward_second_matrix = gaussian(keys[13], (FF, C), (FF // 2) ** -0.5, 0.25)
    feedforward_second_offset = gaussian(keys[14], (C,), 0.3, 2.0, jnp.float32)
    return {"alignment_tensor": alignment_tensor, "standardizer_factors": standardizer_factors, "standardizer_offsets": standardizer_offsets, "horizontal_entry_matrix": horizontal_entry_matrix, "horizontal_sigmoid_offset": horizontal_sigmoid_offset, "horizontal_exit_matrix": horizontal_exit_matrix, "horizontal_exit_offset": horizontal_exit_offset, "vertical_entry_matrix": vertical_entry_matrix, "vertical_sigmoid_offset": vertical_sigmoid_offset, "vertical_exit_matrix": vertical_exit_matrix, "vertical_exit_offset": vertical_exit_offset, "feedforward_first_matrix": feedforward_first_matrix, "feedforward_first_offset": feedforward_first_offset, "feedforward_second_matrix": feedforward_second_matrix, "feedforward_second_offset": feedforward_second_offset}


def standardize_features(values, gain, shift):
    row_mean = lax.optimization_barrier(jnp.mean(values, axis=-1, keepdims=True))
    centred = values - row_mean
    variance = lax.optimization_barrier(jnp.mean(centred * centred, axis=-1, keepdims=True))
    return (centred * lax.rsqrt(variance + 1e-05) * gain + shift).astype(jnp.bfloat16)

def final_mapping(source, weight, offset):
    dims_in = source.shape
    flat = jnp.dot(source.reshape(-1, dims_in[-1]), weight, preferred_element_type=jnp.float32) + offset
    return flat.reshape(dims_in[:-1] + (weight.shape[1],))

def attention_single(normed, proj, gate_bias):
    length, channels = normed.shape
    head_size = channels // HEADS
    projected = jnp.dot(normed, proj, preferred_element_type=jnp.float32)
    query = (projected[:, :channels] * head_size ** (-0.5)).astype(jnp.bfloat16)
    key_rows = projected[:, channels:2 * channels].astype(jnp.bfloat16)
    value_rows = projected[:, 2 * channels:3 * channels].astype(jnp.bfloat16)
    gate_value = jax.nn.sigmoid(projected[:, 3 * channels:] + gate_bias)
    query_f = query.astype(jnp.float32).reshape(length, HEADS, head_size)
    key_f = key_rows.astype(jnp.float32).reshape(length, HEADS, head_size)
    value_f = value_rows.astype(jnp.float32).reshape(length, HEADS, head_size)
    scores = jnp.einsum('qhd,khd->hqk', query_f, key_f, precision=lax.Precision.HIGHEST)
    peak_score = lax.optimization_barrier(jnp.max(scores, axis=-1, keepdims=True))
    weights = jnp.exp(scores - peak_score)
    row_total = lax.optimization_barrier(jnp.sum(weights, axis=-1, keepdims=True))
    probabilities = (weights / row_total).astype(jnp.bfloat16).astype(jnp.float32)
    mixed = jnp.einsum('hqk,khd->qhd', probabilities, value_f, precision=lax.Precision.HIGHEST)
    return (gate_value * mixed.reshape(length, channels)).astype(jnp.bfloat16)

def reference(alignment_tensor, standardizer_factors, standardizer_offsets, horizontal_entry_matrix, horizontal_sigmoid_offset, horizontal_exit_matrix, horizontal_exit_offset, vertical_entry_matrix, vertical_sigmoid_offset, vertical_exit_matrix, vertical_exit_offset, feedforward_first_matrix, feedforward_first_offset, feedforward_second_matrix, feedforward_second_offset):
    standardized_horizontal = standardize_features(alignment_tensor, standardizer_factors[0], standardizer_offsets[0])
    horizontal_sigmoid_masked = lax.map(lambda lone_alignment_entry: attention_single(lone_alignment_entry, horizontal_entry_matrix, horizontal_sigmoid_offset), standardized_horizontal)
    alignment_horizontal_done = alignment_tensor + lax.map(lambda lone_alignment_entry: final_mapping(lone_alignment_entry, horizontal_exit_matrix, horizontal_exit_offset), horizontal_sigmoid_masked)
    standardized_vertical = standardize_features(alignment_horizontal_done, standardizer_factors[1], standardizer_offsets[1]).transpose(1, 0, 2)
    vertical_sigmoid_masked = lax.map(lambda lone_alignment_entry: attention_single(lone_alignment_entry, vertical_entry_matrix, vertical_sigmoid_offset), standardized_vertical).transpose(1, 0, 2)
    vertical_done = alignment_horizontal_done + lax.map(lambda lone_alignment_entry: final_mapping(lone_alignment_entry, vertical_exit_matrix, vertical_exit_offset), vertical_sigmoid_masked)

    def transition(lone_alignment_entry):
        normed_trans = standardize_features(lone_alignment_entry, standardizer_factors[2], standardizer_offsets[2])
        inner = jax.nn.relu(final_mapping(normed_trans, feedforward_first_matrix, feedforward_first_offset)).astype(jnp.bfloat16)
        return lone_alignment_entry + final_mapping(inner, feedforward_second_matrix, feedforward_second_offset)
    return lax.map(transition, vertical_done)
```

```python
import functools

import jax
import jax.numpy as jnp
from jax import lax
from jax.experimental import pallas as pl
from jax.experimental.pallas import tpu as pltpu
from jax.sharding import PartitionSpec as P

HEADS = 8
EPS = 1e-05
F32 = jnp.float32
BF16 = jnp.bfloat16
MESH = pl.DeviceIdType.MESH


def standardize(values, gain, shift):
    mean = jnp.mean(values, axis=-1, keepdims=True)
    centred = values - mean
    variance = jnp.mean(centred * centred, axis=-1, keepdims=True)
    return (centred * lax.rsqrt(variance + EPS) * gain + shift).astype(BF16)


def dot(left, right):
    return jnp.dot(left, right, preferred_element_type=F32)


def dot_nt(left, right):
    return lax.dot_general(left, right, (((1,), (1,)), ((), ())), preferred_element_type=F32)


def attend(normed, entry, value_turned, gate_offset, exit_matrix, mixed):
    length, channels = normed.shape
    size = channels // HEADS
    query = (dot(normed, entry[:, :channels]) * size ** (-0.5)).astype(BF16)
    key = dot(normed, entry[:, channels : 2 * channels]).astype(BF16)
    value = dot_nt(value_turned, normed).astype(BF16)
    gate = jax.nn.sigmoid(dot(normed, entry[:, 3 * channels :]) + gate_offset)
    lane = lax.broadcasted_iota(jnp.int32, (1, channels), 1)

    def one_head(head, own_values):
        low = head * size
        mask = jnp.where((lane >= low) & (lane < low + size), 1.0, 0.0).astype(BF16)
        scores = dot_nt(key * mask, query)
        weights = jnp.exp(scores - jnp.max(scores, axis=0, keepdims=True))
        total = jnp.sum(weights, axis=0, keepdims=True)
        return dot(own_values, weights.astype(BF16)) / total

    if length <= 256:
        outs = [one_head(h, value[h * size : (h + 1) * size]) for h in range(HEADS)]
        turned = jnp.concatenate(outs, axis=0)
    else:
        held, out = mixed
        held[...] = value

        def step(head, carry):
            rows = pl.ds(pl.multiple_of(head * size, size), size)
            out[rows, :] = one_head(head, held[rows, :])
            return carry

        lax.fori_loop(0, HEADS, step, 0)
        turned = out[...]
    gated = (gate * turned.T).astype(BF16)
    return dot(gated, exit_matrix)


def block(
    res_count,
    seq_count,
    x_ref,
    gains,
    shifts,
    row_gate,
    row_shift,
    col_gate,
    col_shift,
    ff_first_shift,
    ff_second_shift,
    row_entry_hbm,
    row_exit_hbm,
    col_entry_hbm,
    col_exit_hbm,
    ff_first_hbm,
    ff_second_hbm,
    out_ref,
    row_entry,
    row_exit,
    col_entry,
    col_exit,
    ff_first,
    ff_second,
    turned_value,
    row_sent,
    row_in,
    row_out,
    row_back,
    after_row,
    after_turned,
    col_sent,
    col_in,
    col_out,
    col_back,
    mixed_row,
    mixed_col,
    load_sem,
    sems,
    col_sems,
):
    me_res = lax.axis_index("res")
    me_seq = lax.axis_index("seq")
    groups, group = x_ref.shape[1], x_ref.shape[2]
    res_local, channels = x_ref.shape[3], x_ref.shape[4]
    seq_local = after_row.shape[0]
    items = groups * group
    columns = res_local // seq_count

    loads = [
        pltpu.make_async_copy(src, dst, load_sem.at[i])
        for i, (src, dst) in enumerate(
            (
                (row_entry_hbm, row_entry),
                (row_exit_hbm, row_exit),
                (col_entry_hbm, col_entry),
                (col_exit_hbm, col_exit),
                (ff_first_hbm, ff_first),
                (ff_second_hbm, ff_second),
            )
        )
    ]
    for load in loads:
        load.start()

    barrier = pltpu.get_barrier_semaphore()

    def greet(axis, me, count):
        def step(k, carry):
            peer = lax.rem(me + k, count)
            pl.semaphore_signal(barrier, inc=1, device_id={axis: peer}, device_id_type=MESH)
            return carry

        lax.fori_loop(1, count, step, 0)

    greet("res", me_res, res_count)
    greet("seq", me_seq, seq_count)

    def send(g, k, src, dst, axis, peer, sem, phase):
        return pltpu.make_async_remote_copy(
            src_ref=src,
            dst_ref=dst,
            send_sem=sem.at[phase, 0, g, k],
            recv_sem=sem.at[phase, 1, g, k],
            device_id={axis: peer},
            device_id_type=MESH,
        )

    def row_copy(g, k):
        peer = lax.rem(me_res + k, res_count)
        return send(g, k, row_sent.at[g, peer], row_in.at[g, me_res], "res", peer, sems, 0)

    def row_return(g, k):
        peer = lax.rem(me_res + k, res_count)
        return send(g, k, row_out.at[g, peer], row_back.at[me_res, g], "res", peer, sems, 1)

    def col_copy(g, k):
        peer = lax.rem(me_seq + k, seq_count)
        return send(
            g, k, col_sent.at[peer * columns + g], col_in.at[g, me_seq], "seq", peer, col_sems, 0
        )

    def col_return(g, k):
        peer = lax.rem(me_seq + k, seq_count)
        return send(
            g, k, col_out.at[g, peer], col_back.at[me_seq * columns + g], "seq", peer, col_sems, 1
        )

    def each(count, act):
        def step(k, carry):
            act(k)
            return carry

        lax.fori_loop(1, count, step, 0)

    for g in range(groups):
        row_sent[g] = standardize(x_ref[:, g], gains[0:1], shifts[0:1])
        if g == 0:
            pl.semaphore_wait(barrier, res_count + seq_count - 2)
        each(res_count, lambda k: row_copy(g, k).start())
        row_in[g, me_res] = row_sent[g, me_res]

    loads[0].wait()
    loads[1].wait()
    turned_value[0] = row_entry[:, 2 * channels : 3 * channels].T
    for g in range(groups):
        each(res_count, lambda k: row_copy(g, k).wait_recv())
        for i in range(group):
            result = attend(
                row_in[g, :, i].reshape(res_count * res_local, channels),
                row_entry,
                turned_value[0],
                row_gate[...],
                row_exit[...],
                mixed_row,
            )
            row_out[g, :, i] = result.astype(BF16).reshape(res_count, res_local, channels)
        each(res_count, lambda k: row_return(g, k).start())
        row_back[me_res, g] = row_out[g, me_res]

    loads[2].wait()
    loads[3].wait()
    turned_value[1] = col_entry[:, 2 * channels : 3 * channels].T
    for g in range(groups):
        each(res_count, lambda k: row_return(g, k).wait_recv())
        for source in range(res_count):
            first = source * items + g * group
            after_row[first : first + group] = (
                x_ref[source, g] + row_back[source, g].astype(F32) + row_shift[...]
            )

    for g in range(columns):
        for part in range(seq_count):
            j = part * columns + g
            here = after_row[:, j, :]
            after_turned[j] = here
            col_sent[j] = standardize(here, gains[1:2], shifts[1:2])
        each(seq_count, lambda k: col_copy(g, k).start())
        col_in[g, me_seq] = col_sent[me_seq * columns + g]

    for g in range(columns):
        each(seq_count, lambda k: col_copy(g, k).wait_recv())
        result = attend(
            col_in[g].reshape(seq_count * seq_local, channels),
            col_entry,
            turned_value[1],
            col_gate[...],
            col_exit[...],
            mixed_col,
        )
        col_out[g] = result.astype(BF16).reshape(seq_count, seq_local, channels)
        each(seq_count, lambda k: col_return(g, k).start())
        col_back[me_seq * columns + g] = col_out[g, me_seq]

    loads[4].wait()
    loads[5].wait()
    for g in range(columns):
        each(seq_count, lambda k: col_return(g, k).wait_recv())
        places = [part * columns + g for part in range(seq_count)]
        done = jnp.concatenate(
            [after_turned[j] + col_back[j].astype(F32) for j in places], axis=0
        ) + col_shift[...]
        normed = standardize(done, gains[2:3], shifts[2:3])
        inner = jnp.maximum(dot(normed, ff_first[...]) + ff_first_shift[...], 0.0).astype(BF16)
        final = done + dot(inner, ff_second[...]) + ff_second_shift[...]
        for part, j in enumerate(places):
            out_ref[:, j, :] = final[part * seq_local : (part + 1) * seq_local]

    for g in range(groups):
        each(res_count, lambda k: row_copy(g, k).wait_send())
        each(res_count, lambda k: row_return(g, k).wait_send())
    for g in range(columns):
        each(seq_count, lambda k: col_copy(g, k).wait_send())
        each(seq_count, lambda k: col_return(g, k).wait_send())


def shards(
    alignment_tensor,
    standardizer_factors,
    standardizer_offsets,
    horizontal_entry_matrix,
    horizontal_sigmoid_offset,
    horizontal_exit_matrix,
    horizontal_exit_offset,
    vertical_entry_matrix,
    vertical_sigmoid_offset,
    vertical_exit_matrix,
    vertical_exit_offset,
    feedforward_first_matrix,
    feedforward_first_offset,
    feedforward_second_matrix,
    feedforward_second_offset,
):
    seq_local, res_local, channels = alignment_tensor.shape
    hidden = feedforward_first_matrix.shape[1]
    res_count = lax.axis_size("res")
    seq_count = lax.axis_size("seq")
    items = seq_local // res_count
    group = 2 if items % 2 == 0 else 1
    groups = items // group
    columns = res_local // seq_count
    vmem = pl.BlockSpec(memory_space=pltpu.VMEM)
    anywhere = pl.BlockSpec(memory_space=pl.ANY)
    row_length, col_length = res_local * res_count, seq_local * seq_count

    def line(vector):
        return vector.reshape(1, -1)

    def mixed(length):
        rows = channels if length > 256 else 16
        wide = length if length > 256 else 128
        return [pltpu.VMEM((rows, wide), BF16), pltpu.VMEM((rows, wide), F32)]

    tokens = seq_local * res_local
    return pl.pallas_call(
        functools.partial(block, res_count, seq_count),
        out_shape=jax.ShapeDtypeStruct(alignment_tensor.shape, F32),
        in_specs=[vmem] * 9 + [anywhere] * 6,
        out_specs=vmem,
        scratch_shapes=[
            pltpu.VMEM(horizontal_entry_matrix.shape, BF16),
            pltpu.VMEM(horizontal_exit_matrix.shape, BF16),
            pltpu.VMEM(vertical_entry_matrix.shape, BF16),
            pltpu.VMEM(vertical_exit_matrix.shape, BF16),
            pltpu.VMEM(feedforward_first_matrix.shape, BF16),
            pltpu.VMEM(feedforward_second_matrix.shape, BF16),
            pltpu.VMEM((2, channels, channels), BF16),
            pltpu.VMEM((groups, res_count, group, res_local, channels), BF16),
            pltpu.VMEM((groups, res_count, group, res_local, channels), BF16),
            pltpu.VMEM((groups, res_count, group, res_local, channels), BF16),
            pltpu.VMEM((res_count, groups, group, res_local, channels), BF16),
            pltpu.VMEM((seq_local, res_local, channels), F32),
            pltpu.VMEM((res_local, seq_local, channels), F32),
            pltpu.VMEM((res_local, seq_local, channels), BF16),
            pltpu.VMEM((columns, seq_count, seq_local, channels), BF16),
            pltpu.VMEM((columns, seq_count, seq_local, channels), BF16),
            pltpu.VMEM((res_local, seq_local, channels), BF16),
            mixed(row_length),
            mixed(col_length),
            pltpu.SemaphoreType.DMA((6,)),
            pltpu.SemaphoreType.DMA((2, 2, groups, res_count)),
            pltpu.SemaphoreType.DMA((2, 2, columns, seq_count)),
        ],
        compiler_params=pltpu.CompilerParams(
            collective_id=0, has_side_effects=True, vmem_limit_bytes=48 * 1024 * 1024
        ),
        cost_estimate=pl.CostEstimate(
            flops=2 * tokens * channels * (10 * channels + 2 * hidden),
            bytes_accessed=16 * tokens * channels,
            transcendentals=tokens * HEADS * (row_length + col_length),
        ),
    )(
        alignment_tensor.reshape(res_count, groups, group, res_local, channels),
        standardizer_factors,
        standardizer_offsets,
        line(horizontal_sigmoid_offset),
        line(horizontal_exit_offset),
        line(vertical_sigmoid_offset),
        line(vertical_exit_offset),
        line(feedforward_first_offset),
        line(feedforward_second_offset),
        horizontal_entry_matrix,
        horizontal_exit_matrix,
        vertical_entry_matrix,
        vertical_exit_matrix,
        feedforward_first_matrix,
        feedforward_second_matrix,
    )


def solution(mesh):
    return jax.shard_map(
        shards,
        mesh=mesh,
        in_specs=(P("seq", "res", None),) + (P(),) * 14,
        out_specs=P("seq", "res", None),
        check_vma=False,
    )
```

```python
import functools

import jax
import jax.numpy as jnp
from jax import lax
from jax.experimental import pallas as pl
from jax.experimental.pallas import tpu as pltpu
from jax.sharding import PartitionSpec as P

HEADS = 8
EPS = 1e-05
F32 = jnp.float32
BF16 = jnp.bfloat16
MESH = pl.DeviceIdType.MESH


def standardize(values, gain, shift):
    mean = jnp.mean(values, axis=-1, keepdims=True)
    centred = values - mean
    variance = jnp.mean(centred * centred, axis=-1, keepdims=True)
    return (centred * lax.rsqrt(variance + EPS) * gain + shift).astype(BF16)


def dot(left, right):
    return jnp.dot(left, right, preferred_element_type=F32)


def dot_nt(left, right):
    return lax.dot_general(left, right, (((1,), (1,)), ((), ())), preferred_element_type=F32)


def attend(normed, length, entry, value_turned, gate_offset, exit_matrix, mixed):
    channels = normed.shape[1]
    size = channels // HEADS
    count = normed.shape[0] // length
    query = (dot(normed, entry[:, :channels]) * size ** (-0.5)).astype(BF16)
    key = dot(normed, entry[:, channels : 2 * channels]).astype(BF16)
    gate = jax.nn.sigmoid(dot(normed, entry[:, 3 * channels :]) + gate_offset)
    spans = [slice(n * length, (n + 1) * length) for n in range(count)]
    values = [dot_nt(value_turned, normed[span]).astype(BF16) for span in spans]
    lane = lax.broadcasted_iota(jnp.int32, (1, channels), 1)

    def mask(head):
        low = head * size
        return jnp.where((lane >= low) & (lane < low + size), 1.0, 0.0).astype(BF16)

    if length <= 256:
        masks = [mask(head) for head in range(HEADS)]
        scores = [
            dot_nt(jnp.concatenate([key[span] * m for m in masks], axis=0), query[span])
            for span in spans
        ]
        heads = [
            (value[h * size : (h + 1) * size], score[h * length : (h + 1) * length])
            for value, score in zip(values, scores)
            for h in range(HEADS)
        ]
        peaks = [jnp.max(score, axis=0, keepdims=True) for _, score in heads]
        weights = [jnp.exp(score - peak) for (_, score), peak in zip(heads, peaks)]
        totals = [jnp.sum(weight, axis=0, keepdims=True) for weight in weights]
        outs = [
            dot(value, weight.astype(BF16)) / total
            for (value, _), weight, total in zip(heads, weights, totals)
        ]
        turned = [
            jnp.concatenate(outs[n * HEADS : (n + 1) * HEADS], axis=0).T for n in range(count)
        ]
    else:
        held, out = mixed
        turned = []
        for span, value in zip(spans, values):
            held[...] = value

            def step(head, carry):
                rows = pl.ds(pl.multiple_of(head * size, size), size)
                score = dot_nt(key[span] * mask(head), query[span])
                weight = jnp.exp(score - jnp.max(score, axis=0, keepdims=True))
                total = jnp.sum(weight, axis=0, keepdims=True)
                out[rows, :] = dot(held[rows, :], weight.astype(BF16)) / total
                return carry

            lax.fori_loop(0, HEADS, step, 0)
            turned.append(out[...].T)
    gated = (gate * jnp.concatenate(turned, axis=0)).astype(BF16)
    return dot(gated, exit_matrix)


def block(
    res_count,
    seq_count,
    x_hbm,
    gains_hbm,
    shifts_hbm,
    row_gate_hbm,
    row_shift_hbm,
    col_gate_hbm,
    col_shift_hbm,
    ff_first_shift_hbm,
    ff_second_shift_hbm,
    row_entry_hbm,
    row_exit_hbm,
    col_entry_hbm,
    col_exit_hbm,
    ff_first_hbm,
    ff_second_hbm,
    out_ref,
    x_ref,
    gains,
    shifts,
    row_gate,
    row_shift,
    col_gate,
    col_shift,
    ff_first_shift,
    ff_second_shift,
    row_entry,
    row_exit,
    col_entry,
    col_exit,
    ff_first,
    ff_second,
    turned_value,
    row_sent,
    row_in,
    row_out,
    row_back,
    after_row,
    after_turned,
    col_sent,
    col_in,
    col_out,
    col_back,
    mixed_row,
    mixed_col,
    x_sem,
    load_sem,
    sems,
    col_sems,
):
    me_res = lax.axis_index("res")
    me_seq = lax.axis_index("seq")
    groups, group = x_ref.shape[1], x_ref.shape[2]
    res_local, channels = x_ref.shape[3], x_ref.shape[4]
    seq_local = after_row.shape[0]
    items = groups * group
    row_length = res_count * res_local
    columns = res_local // seq_count

    barrier = pltpu.get_barrier_semaphore()

    def greet(axis, me, count):
        def step(k, carry):
            peer = lax.rem(me + k, count)
            pl.semaphore_signal(barrier, inc=1, device_id={axis: peer}, device_id_type=MESH)
            return carry

        lax.fori_loop(1, count, step, 0)

    greet("res", me_res, res_count)
    greet("seq", me_seq, seq_count)

    x_loads = [
        pltpu.make_async_copy(x_hbm.at[:, g], x_ref.at[:, g], x_sem.at[g]) for g in range(groups)
    ]
    pairs = (
        (gains_hbm, gains),
        (shifts_hbm, shifts),
        (row_gate_hbm, row_gate),
        (row_shift_hbm, row_shift),
        (col_gate_hbm, col_gate),
        (col_shift_hbm, col_shift),
        (ff_first_shift_hbm, ff_first_shift),
        (ff_second_shift_hbm, ff_second_shift),
        (row_entry_hbm, row_entry),
        (row_exit_hbm, row_exit),
        (col_entry_hbm, col_entry),
        (col_exit_hbm, col_exit),
        (ff_first_hbm, ff_first),
        (ff_second_hbm, ff_second),
    )
    loads = [
        pltpu.make_async_copy(src, dst, load_sem.at[i]) for i, (src, dst) in enumerate(pairs)
    ]
    for load in loads[:2] + x_loads + loads[2:]:
        load.start()

    def send(g, k, src, dst, axis, peer, sem, phase):
        return pltpu.make_async_remote_copy(
            src_ref=src,
            dst_ref=dst,
            send_sem=sem.at[phase, 0, g, k],
            recv_sem=sem.at[phase, 1, g, k],
            device_id={axis: peer},
            device_id_type=MESH,
        )

    def row_copy(g, k):
        peer = lax.rem(me_res + k, res_count)
        return send(g, k, row_sent.at[g, peer], row_in.at[g, me_res], "res", peer, sems, 0)

    def row_return(g, k):
        peer = lax.rem(me_res + k, res_count)
        return send(g, k, row_out.at[g, peer], row_back.at[me_res, g], "res", peer, sems, 1)

    def col_copy(g, k):
        peer = lax.rem(me_seq + k, seq_count)
        return send(
            g, k, col_sent.at[peer * columns + g], col_in.at[g, me_seq], "seq", peer, col_sems, 0
        )

    def col_return(g, k):
        peer = lax.rem(me_seq + k, seq_count)
        return send(
            g, k, col_out.at[g, peer], col_back.at[me_seq * columns + g], "seq", peer, col_sems, 1
        )

    def each(count, act):
        def step(k, carry):
            act(k)
            return carry

        lax.fori_loop(1, count, step, 0)

    loads[0].wait()
    loads[1].wait()
    for g in range(groups):
        x_loads[g].wait()
        row_sent[g] = standardize(x_ref[:, g], gains[0:1], shifts[0:1])
        if g == 0:
            pl.semaphore_wait(barrier, res_count + seq_count - 2)
        each(res_count, lambda k: row_copy(g, k).start())
        row_in[g, me_res] = row_sent[g, me_res]

    for i in (2, 3, 8, 9):
        loads[i].wait()
    turned_value[0] = row_entry[:, 2 * channels : 3 * channels].T
    for g in range(groups):
        each(res_count, lambda k: row_copy(g, k).wait_recv())
        result = attend(
            jnp.concatenate(
                [row_in[g, :, i].reshape(row_length, channels) for i in range(group)], axis=0
            ),
            row_length,
            row_entry,
            turned_value[0],
            row_gate[...],
            row_exit[...],
            mixed_row,
        ).astype(BF16)
        for i in range(group):
            row_out[g, :, i] = result[i * row_length : (i + 1) * row_length].reshape(
                res_count, res_local, channels
            )
        each(res_count, lambda k: row_return(g, k).start())
        row_back[me_res, g] = row_out[g, me_res]

    for i in (4, 5, 10, 11):
        loads[i].wait()
    turned_value[1] = col_entry[:, 2 * channels : 3 * channels].T
    for g in range(groups):
        each(res_count, lambda k: row_return(g, k).wait_recv())
        for source in range(res_count):
            first = source * items + g * group
            after_row[first : first + group] = (
                x_ref[source, g] + row_back[source, g].astype(F32) + row_shift[...]
            )

    for g in range(columns):
        for part in range(seq_count):
            j = part * columns + g
            here = after_row[:, j, :]
            after_turned[j] = here
            col_sent[j] = standardize(here, gains[1:2], shifts[1:2])
        each(seq_count, lambda k: col_copy(g, k).start())
        col_in[g, me_seq] = col_sent[me_seq * columns + g]

    for g in range(columns):
        each(seq_count, lambda k: col_copy(g, k).wait_recv())
        result = attend(
            col_in[g].reshape(seq_count * seq_local, channels),
            seq_count * seq_local,
            col_entry,
            turned_value[1],
            col_gate[...],
            col_exit[...],
            mixed_col,
        )
        col_out[g] = result.astype(BF16).reshape(seq_count, seq_local, channels)
        each(seq_count, lambda k: col_return(g, k).start())
        col_back[me_seq * columns + g] = col_out[g, me_seq]

    for i in (6, 7, 12, 13):
        loads[i].wait()
    for g in range(columns):
        each(seq_count, lambda k: col_return(g, k).wait_recv())
        places = [part * columns + g for part in range(seq_count)]
        done = jnp.concatenate(
            [after_turned[j] + col_back[j].astype(F32) for j in places], axis=0
        ) + col_shift[...]
        normed = standardize(done, gains[2:3], shifts[2:3])
        inner = jnp.maximum(dot(normed, ff_first[...]) + ff_first_shift[...], 0.0).astype(BF16)
        final = done + dot(inner, ff_second[...]) + ff_second_shift[...]
        for part, j in enumerate(places):
            out_ref[:, j, :] = final[part * seq_local : (part + 1) * seq_local]

    for g in range(groups):
        each(res_count, lambda k: row_copy(g, k).wait_send())
        each(res_count, lambda k: row_return(g, k).wait_send())
    for g in range(columns):
        each(seq_count, lambda k: col_copy(g, k).wait_send())
        each(seq_count, lambda k: col_return(g, k).wait_send())


def shards(
    alignment_tensor,
    standardizer_factors,
    standardizer_offsets,
    horizontal_entry_matrix,
    horizontal_sigmoid_offset,
    horizontal_exit_matrix,
    horizontal_exit_offset,
    vertical_entry_matrix,
    vertical_sigmoid_offset,
    vertical_exit_matrix,
    vertical_exit_offset,
    feedforward_first_matrix,
    feedforward_first_offset,
    feedforward_second_matrix,
    feedforward_second_offset,
):
    seq_local, res_local, channels = alignment_tensor.shape
    hidden = feedforward_first_matrix.shape[1]
    res_count = lax.axis_size("res")
    seq_count = lax.axis_size("seq")
    items = seq_local // res_count
    group = 2 if items % 2 == 0 else 1
    groups = items // group
    columns = res_local // seq_count
    vmem = pl.BlockSpec(memory_space=pltpu.VMEM)
    in_hbm = pl.BlockSpec(memory_space=pltpu.HBM)
    row_length, col_length = res_local * res_count, seq_local * seq_count

    def line(vector):
        return vector.reshape(1, -1)

    def mixed(length):
        rows = channels if length > 256 else 16
        wide = length if length > 256 else 128
        return [pltpu.VMEM((rows, wide), BF16), pltpu.VMEM((rows, wide), F32)]

    tokens = seq_local * res_local
    return pl.pallas_call(
        functools.partial(block, res_count, seq_count),
        out_shape=jax.ShapeDtypeStruct(alignment_tensor.shape, F32),
        in_specs=[in_hbm] * 15,
        out_specs=vmem,
        scratch_shapes=[
            pltpu.VMEM((res_count, groups, group, res_local, channels), F32),
            pltpu.VMEM(standardizer_factors.shape, F32),
            pltpu.VMEM(standardizer_offsets.shape, F32),
            pltpu.VMEM((1, channels), F32),
            pltpu.VMEM((1, channels), F32),
            pltpu.VMEM((1, channels), F32),
            pltpu.VMEM((1, channels), F32),
            pltpu.VMEM((1, hidden), F32),
            pltpu.VMEM((1, channels), F32),
            pltpu.VMEM(horizontal_entry_matrix.shape, BF16),
            pltpu.VMEM(horizontal_exit_matrix.shape, BF16),
            pltpu.VMEM(vertical_entry_matrix.shape, BF16),
            pltpu.VMEM(vertical_exit_matrix.shape, BF16),
            pltpu.VMEM(feedforward_first_matrix.shape, BF16),
            pltpu.VMEM(feedforward_second_matrix.shape, BF16),
            pltpu.VMEM((2, channels, channels), BF16),
            pltpu.VMEM((groups, res_count, group, res_local, channels), BF16),
            pltpu.VMEM((groups, res_count, group, res_local, channels), BF16),
            pltpu.VMEM((groups, res_count, group, res_local, channels), BF16),
            pltpu.VMEM((res_count, groups, group, res_local, channels), BF16),
            pltpu.VMEM((seq_local, res_local, channels), F32),
            pltpu.VMEM((res_local, seq_local, channels), F32),
            pltpu.VMEM((res_local, seq_local, channels), BF16),
            pltpu.VMEM((columns, seq_count, seq_local, channels), BF16),
            pltpu.VMEM((columns, seq_count, seq_local, channels), BF16),
            pltpu.VMEM((res_local, seq_local, channels), BF16),
            mixed(row_length),
            mixed(col_length),
            pltpu.SemaphoreType.DMA((groups,)),
            pltpu.SemaphoreType.DMA((14,)),
            pltpu.SemaphoreType.DMA((2, 2, groups, res_count)),
            pltpu.SemaphoreType.DMA((2, 2, columns, seq_count)),
        ],
        compiler_params=pltpu.CompilerParams(
            collective_id=0, has_side_effects=True, vmem_limit_bytes=63 * 1024 * 1024
        ),
        cost_estimate=pl.CostEstimate(
            flops=2 * tokens * channels * (10 * channels + 2 * hidden),
            bytes_accessed=16 * tokens * channels,
            transcendentals=tokens * HEADS * (row_length + col_length),
        ),
    )(
        alignment_tensor.reshape(res_count, groups, group, res_local, channels),
        standardizer_factors,
        standardizer_offsets,
        line(horizontal_sigmoid_offset),
        line(horizontal_exit_offset),
        line(vertical_sigmoid_offset),
        line(vertical_exit_offset),
        line(feedforward_first_offset),
        line(feedforward_second_offset),
        horizontal_entry_matrix,
        horizontal_exit_matrix,
        vertical_entry_matrix,
        vertical_exit_matrix,
        feedforward_first_matrix,
        feedforward_second_matrix,
    )


def solution(mesh):
    return jax.shard_map(
        shards,
        mesh=mesh,
        in_specs=(P("seq", "res", None),) + (P(),) * 14,
        out_specs=P("seq", "res", None),
        check_vma=False,
    )
```

```python
import functools

import jax
import jax.numpy as jnp
from jax import lax
from jax.experimental import pallas as pl
from jax.experimental.pallas import tpu as pltpu
from jax.sharding import PartitionSpec as P

HEADS = 8
EPS = 1e-05
F32 = jnp.float32
BF16 = jnp.bfloat16
MESH = pl.DeviceIdType.MESH


def standardize(values, gain, shift):
    mean = jnp.mean(values, axis=-1, keepdims=True)
    centred = values - mean
    variance = jnp.mean(centred * centred, axis=-1, keepdims=True)
    return (centred * lax.rsqrt(variance + EPS) * gain + shift).astype(BF16)


def dot(left, right):
    return jnp.dot(left, right, preferred_element_type=F32)


def dot_nt(left, right):
    return lax.dot_general(left, right, (((1,), (1,)), ((), ())), preferred_element_type=F32)


def attend(normed, length, entry, value_turned, gate_offset, exit_matrix, mixed):
    channels = normed.shape[1]
    size = channels // HEADS
    count = normed.shape[0] // length
    query = (dot(normed, entry[:, :channels]) * size ** (-0.5)).astype(BF16)
    key = dot(normed, entry[:, channels : 2 * channels]).astype(BF16)
    gate = jax.nn.sigmoid(dot(normed, entry[:, 3 * channels :]) + gate_offset)
    spans = [slice(n * length, (n + 1) * length) for n in range(count)]
    value = dot_nt(value_turned, normed).astype(BF16)
    values = [value[:, span] for span in spans]
    ones = jnp.ones((16, length), BF16)
    lane = lax.broadcasted_iota(jnp.int32, (1, channels), 1)

    def weigh(score, value):
        weight = jnp.exp((score - jnp.max(score, axis=0, keepdims=True)).astype(BF16))
        return dot(jnp.concatenate([value, ones], axis=0), weight)

    def share(product):
        return product[:size] * (1.0 / product[size : size + 1])

    def mask(head):
        low = head * size
        return jnp.where((lane >= low) & (lane < low + size), 1.0, 0.0).astype(BF16)

    if length <= 256:
        masks = [mask(head) for head in range(HEADS)]
        scores = [
            dot_nt(jnp.concatenate([key[span] * m for m in masks], axis=0), query[span])
            for span in spans
        ]
        heads = [
            (value[h * size : (h + 1) * size], score[h * length : (h + 1) * length])
            for value, score in zip(values, scores)
            for h in range(HEADS)
        ]
        outs = [share(product) for product in [weigh(score, value) for value, score in heads]]
        turned = [
            jnp.concatenate(outs[n * HEADS : (n + 1) * HEADS], axis=0).T for n in range(count)
        ]
    else:
        held, out = mixed
        turned = []
        for span, value in zip(spans, values):
            held[...] = value

            def step(head, carry):
                rows = pl.ds(pl.multiple_of(head * size, size), size)
                score = dot_nt(key[span] * mask(head), query[span])
                out[rows, :] = share(weigh(score, held[rows, :]))
                return carry

            lax.fori_loop(0, HEADS, step, 0)
            turned.append(out[...].T)
    gated = (gate * jnp.concatenate(turned, axis=0)).astype(BF16)
    return dot(gated, exit_matrix)


def block(
    res_count,
    seq_count,
    x_hbm,
    gains_hbm,
    shifts_hbm,
    row_gate_hbm,
    row_shift_hbm,
    col_gate_hbm,
    col_shift_hbm,
    ff_first_shift_hbm,
    ff_second_shift_hbm,
    row_entry_hbm,
    row_exit_hbm,
    col_entry_hbm,
    col_exit_hbm,
    ff_first_hbm,
    ff_second_hbm,
    out_ref,
    x_ref,
    gains,
    shifts,
    row_gate,
    row_shift,
    col_gate,
    col_shift,
    ff_first_shift,
    ff_second_shift,
    row_entry,
    row_exit,
    col_entry,
    col_exit,
    ff_first,
    ff_second,
    turned_value,
    row_sent,
    row_in,
    row_out,
    row_back,
    after_row,
    after_turned,
    col_sent,
    col_in,
    col_out,
    col_back,
    mixed_row,
    mixed_col,
    x_sem,
    load_sem,
    sems,
    col_sems,
):
    me_res = lax.axis_index("res")
    me_seq = lax.axis_index("seq")
    groups, group = x_ref.shape[1], x_ref.shape[2]
    res_local, channels = x_ref.shape[3], x_ref.shape[4]
    seq_local = after_row.shape[0]
    items = groups * group
    row_length = res_count * res_local
    columns = res_local // seq_count

    barrier = pltpu.get_barrier_semaphore()

    def greet(axis, me, count):
        def step(k, carry):
            peer = lax.rem(me + k, count)
            pl.semaphore_signal(barrier, inc=1, device_id={axis: peer}, device_id_type=MESH)
            return carry

        lax.fori_loop(1, count, step, 0)

    greet("res", me_res, res_count)
    greet("seq", me_seq, seq_count)

    x_loads = [
        pltpu.make_async_copy(x_hbm.at[:, g], x_ref.at[:, g], x_sem.at[g]) for g in range(groups)
    ]
    pairs = (
        (gains_hbm, gains),
        (shifts_hbm, shifts),
        (row_gate_hbm, row_gate),
        (row_shift_hbm, row_shift),
        (col_gate_hbm, col_gate),
        (col_shift_hbm, col_shift),
        (ff_first_shift_hbm, ff_first_shift),
        (ff_second_shift_hbm, ff_second_shift),
        (row_entry_hbm, row_entry),
        (row_exit_hbm, row_exit),
        (col_entry_hbm, col_entry),
        (col_exit_hbm, col_exit),
        (ff_first_hbm, ff_first),
        (ff_second_hbm, ff_second),
    )
    loads = [
        pltpu.make_async_copy(src, dst, load_sem.at[i]) for i, (src, dst) in enumerate(pairs)
    ]
    for load in loads[:2] + x_loads + loads[2:]:
        load.start()

    def send(g, k, src, dst, axis, peer, sem, phase):
        return pltpu.make_async_remote_copy(
            src_ref=src,
            dst_ref=dst,
            send_sem=sem.at[phase, 0, g, k],
            recv_sem=sem.at[phase, 1, g, k],
            device_id={axis: peer},
            device_id_type=MESH,
        )

    def row_copy(g, k):
        peer = lax.rem(me_res + k, res_count)
        return send(g, k, row_sent.at[g, peer], row_in.at[g, me_res], "res", peer, sems, 0)

    def row_return(g, k):
        peer = lax.rem(me_res + k, res_count)
        return send(g, k, row_out.at[g, peer], row_back.at[me_res, g], "res", peer, sems, 1)

    def col_copy(g, k):
        peer = lax.rem(me_seq + k, seq_count)
        return send(
            g, k, col_sent.at[peer * columns + g], col_in.at[g, me_seq], "seq", peer, col_sems, 0
        )

    def col_return(g, k):
        peer = lax.rem(me_seq + k, seq_count)
        return send(
            g, k, col_out.at[g, peer], col_back.at[me_seq * columns + g], "seq", peer, col_sems, 1
        )

    def each(count, act):
        def step(k, carry):
            act(k)
            return carry

        lax.fori_loop(1, count, step, 0)

    loads[0].wait()
    loads[1].wait()
    for g in range(groups):
        x_loads[g].wait()
        row_sent[g] = standardize(x_ref[:, g], gains[0:1], shifts[0:1])
        if g == 0:
            pl.semaphore_wait(barrier, res_count + seq_count - 2)
        each(res_count, lambda k: row_copy(g, k).start())
        row_in[g, me_res] = row_sent[g, me_res]

    for i in (2, 3, 8, 9):
        loads[i].wait()
    turned_value[0] = row_entry[:, 2 * channels : 3 * channels].T
    for g in range(groups):
        each(res_count, lambda k: row_copy(g, k).wait_recv())
        result = attend(
            jnp.concatenate(
                [row_in[g, :, i].reshape(row_length, channels) for i in range(group)], axis=0
            ),
            row_length,
            row_entry,
            turned_value[0],
            row_gate[...],
            row_exit[...],
            mixed_row,
        ).astype(BF16)
        for i in range(group):
            row_out[g, :, i] = result[i * row_length : (i + 1) * row_length].reshape(
                res_count, res_local, channels
            )
        each(res_count, lambda k: row_return(g, k).start())
        row_back[me_res, g] = row_out[g, me_res]

    for i in (4, 5, 10, 11):
        loads[i].wait()
    turned_value[1] = col_entry[:, 2 * channels : 3 * channels].T
    for g in range(groups):
        each(res_count, lambda k: row_return(g, k).wait_recv())
        for source in range(res_count):
            first = source * items + g * group
            after_row[first : first + group] = (
                x_ref[source, g] + row_back[source, g].astype(F32) + row_shift[...]
            )

    for g in range(columns):
        for part in range(seq_count):
            j = part * columns + g
            here = after_row[:, j, :]
            after_turned[j] = here
            col_sent[j] = standardize(here, gains[1:2], shifts[1:2])
        each(seq_count, lambda k: col_copy(g, k).start())
        col_in[g, me_seq] = col_sent[me_seq * columns + g]

    for g in range(columns):
        each(seq_count, lambda k: col_copy(g, k).wait_recv())
        result = attend(
            col_in[g].reshape(seq_count * seq_local, channels),
            seq_count * seq_local,
            col_entry,
            turned_value[1],
            col_gate[...],
            col_exit[...],
            mixed_col,
        )
        col_out[g] = result.astype(BF16).reshape(seq_count, seq_local, channels)
        each(seq_count, lambda k: col_return(g, k).start())
        col_back[me_seq * columns + g] = col_out[g, me_seq]

    for i in (6, 7, 12, 13):
        loads[i].wait()
    for g in range(columns):
        each(seq_count, lambda k: col_return(g, k).wait_recv())
        places = [part * columns + g for part in range(seq_count)]
        done = jnp.concatenate(
            [after_turned[j] + col_back[j].astype(F32) for j in places], axis=0
        ) + col_shift[...]
        normed = standardize(done, gains[2:3], shifts[2:3])
        inner = jnp.maximum(dot(normed, ff_first[...]) + ff_first_shift[...], 0.0).astype(BF16)
        final = done + dot(inner, ff_second[...]) + ff_second_shift[...]
        for part, j in enumerate(places):
            out_ref[:, j, :] = final[part * seq_local : (part + 1) * seq_local]

    for g in range(groups):
        each(res_count, lambda k: row_copy(g, k).wait_send())
        each(res_count, lambda k: row_return(g, k).wait_send())
    for g in range(columns):
        each(seq_count, lambda k: col_copy(g, k).wait_send())
        each(seq_count, lambda k: col_return(g, k).wait_send())


def shards(
    alignment_tensor,
    standardizer_factors,
    standardizer_offsets,
    horizontal_entry_matrix,
    horizontal_sigmoid_offset,
    horizontal_exit_matrix,
    horizontal_exit_offset,
    vertical_entry_matrix,
    vertical_sigmoid_offset,
    vertical_exit_matrix,
    vertical_exit_offset,
    feedforward_first_matrix,
    feedforward_first_offset,
    feedforward_second_matrix,
    feedforward_second_offset,
):
    seq_local, res_local, channels = alignment_tensor.shape
    hidden = feedforward_first_matrix.shape[1]
    res_count = lax.axis_size("res")
    seq_count = lax.axis_size("seq")
    items = seq_local // res_count
    group = 2 if items % 2 == 0 else 1
    groups = items // group
    columns = res_local // seq_count
    vmem = pl.BlockSpec(memory_space=pltpu.VMEM)
    in_hbm = pl.BlockSpec(memory_space=pltpu.HBM)
    row_length, col_length = res_local * res_count, seq_local * seq_count

    def line(vector):
        return vector.reshape(1, -1)

    def mixed(length):
        rows = channels if length > 256 else 16
        wide = length if length > 256 else 128
        return [pltpu.VMEM((rows, wide), BF16), pltpu.VMEM((rows, wide), F32)]

    tokens = seq_local * res_local
    return pl.pallas_call(
        functools.partial(block, res_count, seq_count),
        out_shape=jax.ShapeDtypeStruct(alignment_tensor.shape, F32),
        in_specs=[in_hbm] * 15,
        out_specs=vmem,
        scratch_shapes=[
            pltpu.VMEM((res_count, groups, group, res_local, channels), F32),
            pltpu.VMEM(standardizer_factors.shape, F32),
            pltpu.VMEM(standardizer_offsets.shape, F32),
            pltpu.VMEM((1, channels), F32),
            pltpu.VMEM((1, channels), F32),
            pltpu.VMEM((1, channels), F32),
            pltpu.VMEM((1, channels), F32),
            pltpu.VMEM((1, hidden), F32),
            pltpu.VMEM((1, channels), F32),
            pltpu.VMEM(horizontal_entry_matrix.shape, BF16),
            pltpu.VMEM(horizontal_exit_matrix.shape, BF16),
            pltpu.VMEM(vertical_entry_matrix.shape, BF16),
            pltpu.VMEM(vertical_exit_matrix.shape, BF16),
            pltpu.VMEM(feedforward_first_matrix.shape, BF16),
            pltpu.VMEM(feedforward_second_matrix.shape, BF16),
            pltpu.VMEM((2, channels, channels), BF16),
            pltpu.VMEM((groups, res_count, group, res_local, channels), BF16),
            pltpu.VMEM((groups, res_count, group, res_local, channels), BF16),
            pltpu.VMEM((groups, res_count, group, res_local, channels), BF16),
            pltpu.VMEM((res_count, groups, group, res_local, channels), BF16),
            pltpu.VMEM((seq_local, res_local, channels), F32),
            pltpu.VMEM((res_local, seq_local, channels), F32),
            pltpu.VMEM((res_local, seq_local, channels), BF16),
            pltpu.VMEM((columns, seq_count, seq_local, channels), BF16),
            pltpu.VMEM((columns, seq_count, seq_local, channels), BF16),
            pltpu.VMEM((res_local, seq_local, channels), BF16),
            mixed(row_length),
            mixed(col_length),
            pltpu.SemaphoreType.DMA((groups,)),
            pltpu.SemaphoreType.DMA((14,)),
            pltpu.SemaphoreType.DMA((2, 2, groups, res_count)),
            pltpu.SemaphoreType.DMA((2, 2, columns, seq_count)),
        ],
        compiler_params=pltpu.CompilerParams(
            collective_id=0, has_side_effects=True, vmem_limit_bytes=63 * 1024 * 1024
        ),
        cost_estimate=pl.CostEstimate(
            flops=2 * tokens * channels * (10 * channels + 2 * hidden),
            bytes_accessed=16 * tokens * channels,
            transcendentals=tokens * HEADS * (row_length + col_length),
        ),
    )(
        alignment_tensor.reshape(res_count, groups, group, res_local, channels),
        standardizer_factors,
        standardizer_offsets,
        line(horizontal_sigmoid_offset),
        line(horizontal_exit_offset),
        line(vertical_sigmoid_offset),
        line(vertical_exit_offset),
        line(feedforward_first_offset),
        line(feedforward_second_offset),
        horizontal_entry_matrix,
        horizontal_exit_matrix,
        vertical_entry_matrix,
        vertical_exit_matrix,
        feedforward_first_matrix,
        feedforward_second_matrix,
    )


def solution(mesh):
    return jax.shard_map(
        shards,
        mesh=mesh,
        in_specs=(P("seq", "res", None),) + (P(),) * 14,
        out_specs=P("seq", "res", None),
        check_vma=False,
    )
```

```python
import functools

import jax
import jax.numpy as jnp
from jax import lax
from jax.experimental import pallas as pl
from jax.experimental.pallas import tpu as pltpu
from jax.sharding import PartitionSpec as P

HEADS = 8
EPS = 1e-05
F32 = jnp.float32
BF16 = jnp.bfloat16
MESH = pl.DeviceIdType.MESH


def standardize(values, gain, shift):
    mean = jnp.mean(values, axis=-1, keepdims=True)
    centred = values - mean
    variance = jnp.mean(centred * centred, axis=-1, keepdims=True)
    return (centred * lax.rsqrt(variance + EPS) * gain + shift).astype(BF16)


def dot(left, right):
    return jnp.dot(left, right, preferred_element_type=F32)


def dot_nt(left, right):
    return lax.dot_general(left, right, (((1,), (1,)), ((), ())), preferred_element_type=F32)


def attend(normed, length, entry, value_turned, gate_offset, exit_matrix, mixed):
    channels = normed.shape[1]
    size = channels // HEADS
    count = normed.shape[0] // length
    query = (dot(normed, entry[:, :channels]) * size ** (-0.5)).astype(BF16)
    key = dot(normed, entry[:, channels : 2 * channels]).astype(BF16)
    gate = jax.nn.sigmoid(dot(normed, entry[:, 3 * channels :]) + gate_offset)
    spans = [slice(n * length, (n + 1) * length) for n in range(count)]
    value = dot_nt(value_turned, normed).astype(BF16)
    values = [value[:, span] for span in spans]
    ones = jnp.ones((16, length), BF16)
    lane = lax.broadcasted_iota(jnp.int32, (1, channels), 1)

    def weigh(score, value):
        weight = jnp.exp((score - jnp.max(score, axis=0, keepdims=True)).astype(BF16))
        return dot(jnp.concatenate([value, ones], axis=0), weight)

    def share(product):
        return product[:size] * (1.0 / product[size : size + 1])

    def mask(head):
        low = head * size
        return jnp.where((lane >= low) & (lane < low + size), 1.0, 0.0).astype(BF16)

    if length <= 256:
        masks = [mask(head) for head in range(HEADS)]
        scores = [
            dot_nt(jnp.concatenate([key[span] * m for m in masks], axis=0), query[span])
            for span in spans
        ]
        heads = [
            (value[h * size : (h + 1) * size], score[h * length : (h + 1) * length])
            for value, score in zip(values, scores)
            for h in range(HEADS)
        ]
        outs = [share(product) for product in [weigh(score, value) for value, score in heads]]
        turned = [
            jnp.concatenate(outs[n * HEADS : (n + 1) * HEADS], axis=0).T for n in range(count)
        ]
    else:
        held, out = mixed
        turned = []
        for span, value in zip(spans, values):
            held[...] = value

            def step(head, carry):
                rows = pl.ds(pl.multiple_of(head * size, size), size)
                score = dot_nt(key[span] * mask(head), query[span])
                out[rows, :] = share(weigh(score, held[rows, :]))
                return carry

            lax.fori_loop(0, HEADS, step, 0)
            turned.append(out[...].T)
    gated = (gate * jnp.concatenate(turned, axis=0)).astype(BF16)
    return dot(gated, exit_matrix)


def block(
    res_count,
    seq_count,
    x_hbm,
    gains_hbm,
    shifts_hbm,
    row_gate_hbm,
    row_shift_hbm,
    col_gate_hbm,
    col_shift_hbm,
    ff_first_shift_hbm,
    ff_second_shift_hbm,
    row_entry_hbm,
    row_exit_hbm,
    col_entry_hbm,
    col_exit_hbm,
    ff_first_hbm,
    ff_second_hbm,
    out_ref,
    x_ref,
    gains,
    shifts,
    row_gate,
    row_shift,
    col_gate,
    col_shift,
    ff_first_shift,
    ff_second_shift,
    row_entry,
    row_exit,
    col_entry,
    col_exit,
    ff_first,
    ff_second,
    turned_value,
    row_sent,
    row_in,
    row_out,
    row_back,
    after_row,
    after_turned,
    col_sent,
    col_in,
    col_out,
    col_back,
    mixed_row,
    mixed_col,
    x_sem,
    load_sem,
    sems,
    back_sems,
    col_sems,
):
    me_res = lax.axis_index("res")
    me_seq = lax.axis_index("seq")
    groups, group = x_ref.shape[1], x_ref.shape[2]
    res_local, channels = x_ref.shape[3], x_ref.shape[4]
    seq_local = after_row.shape[0]
    items = groups * group
    row_length = res_count * res_local
    columns = res_local // seq_count
    halves = row_out.shape[0]
    part_rows, part_columns = res_local // halves, columns // halves

    barrier = pltpu.get_barrier_semaphore()

    def greet(axis, me, count):
        def step(k, carry):
            peer = lax.rem(me + k, count)
            pl.semaphore_signal(barrier, inc=1, device_id={axis: peer}, device_id_type=MESH)
            return carry

        lax.fori_loop(1, count, step, 0)

    greet("res", me_res, res_count)
    greet("seq", me_seq, seq_count)

    x_loads = [
        pltpu.make_async_copy(x_hbm.at[:, g], x_ref.at[:, g], x_sem.at[g]) for g in range(groups)
    ]
    pairs = (
        (gains_hbm, gains),
        (shifts_hbm, shifts),
        (row_gate_hbm, row_gate),
        (row_shift_hbm, row_shift),
        (col_gate_hbm, col_gate),
        (col_shift_hbm, col_shift),
        (ff_first_shift_hbm, ff_first_shift),
        (ff_second_shift_hbm, ff_second_shift),
        (row_entry_hbm, row_entry),
        (row_exit_hbm, row_exit),
        (col_entry_hbm, col_entry),
        (col_exit_hbm, col_exit),
        (ff_first_hbm, ff_first),
        (ff_second_hbm, ff_second),
    )
    loads = [
        pltpu.make_async_copy(src, dst, load_sem.at[i]) for i, (src, dst) in enumerate(pairs)
    ]
    for load in loads[:2] + x_loads + loads[2:]:
        load.start()

    def send(g, k, src, dst, axis, peer, sem, phase):
        return pltpu.make_async_remote_copy(
            src_ref=src,
            dst_ref=dst,
            send_sem=sem.at[phase, 0, g, k],
            recv_sem=sem.at[phase, 1, g, k],
            device_id={axis: peer},
            device_id_type=MESH,
        )

    def row_copy(g, k):
        peer = lax.rem(me_res + k, res_count)
        return send(g, k, row_sent.at[g, peer], row_in.at[g, me_res], "res", peer, sems, 0)

    def row_return(h, g, k):
        peer = lax.rem(me_res + k, res_count)
        return send(
            h * groups + g,
            k,
            row_out.at[h, g, peer],
            row_back.at[h, me_res, g],
            "res",
            peer,
            back_sems,
            0,
        )

    def col_copy(g, k):
        peer = lax.rem(me_seq + k, seq_count)
        return send(
            g, k, col_sent.at[g, peer], col_in.at[g, me_seq], "seq", peer, col_sems, 0
        )

    def col_return(g, k):
        peer = lax.rem(me_seq + k, seq_count)
        return send(
            g, k, col_out.at[g, peer], col_back.at[g, me_seq], "seq", peer, col_sems, 1
        )

    def each(count, act):
        def step(k, carry):
            act(k)
            return carry

        lax.fori_loop(1, count, step, 0)

    loads[0].wait()
    loads[1].wait()
    for g in range(groups):
        x_loads[g].wait()
        row_sent[g] = standardize(x_ref[:, g], gains[0:1], shifts[0:1])
        if g == 0:
            pl.semaphore_wait(barrier, res_count + seq_count - 2)
        each(res_count, lambda k: row_copy(g, k).start())
        row_in[g, me_res] = row_sent[g, me_res]

    for i in (2, 3, 8, 9):
        loads[i].wait()
    turned_value[0] = row_entry[:, 2 * channels : 3 * channels].T
    for g in range(groups):
        each(res_count, lambda k: row_copy(g, k).wait_recv())
        result = attend(
            jnp.concatenate(
                [row_in[g, :, i].reshape(row_length, channels) for i in range(group)], axis=0
            ),
            row_length,
            row_entry,
            turned_value[0],
            row_gate[...],
            row_exit[...],
            mixed_row,
        )
        result = result.reshape(group, res_count, res_local, channels)
        for h in range(halves):
            rows = slice(h * part_rows, (h + 1) * part_rows)
            row_out[h, g] = jnp.concatenate(
                [result[i, :, rows] for i in range(group)], axis=1
            ).astype(BF16)
        each(res_count, lambda k: row_return(0, g, k).start())
        for h in range(1, halves):
            if g > 0:
                each(res_count, lambda k: row_return(h, g - 1, k).start())
            if g == groups - 1:
                each(res_count, lambda k: row_return(h, g, k).start())
        for h in range(halves):
            row_back[h, me_res, g] = row_out[h, g, me_res]

    for i in (4, 5, 10, 11):
        loads[i].wait()
    turned_value[1] = col_entry[:, 2 * channels : 3 * channels].T
    def send_columns(h):
        rows = slice(h * part_rows, (h + 1) * part_rows)
        for g in range(groups):
            each(res_count, lambda k: row_return(h, g, k).wait_recv())
            for source in range(res_count):
                first = source * items + g * group
                back = row_back[h, source, g].astype(F32).reshape(group, part_rows, channels)
                after_row[first : first + group, rows] = (
                    x_ref[source, g, :, rows] + back + row_shift[...]
                )
        for g in range(h * part_columns, (h + 1) * part_columns):
            for part in range(seq_count):
                here = after_row[:, g * seq_count + part, :]
                after_turned[g, part] = here
                col_sent[g, part] = standardize(here, gains[1:2], shifts[1:2])
            each(seq_count, lambda k: col_copy(g, k).start())
            col_in[g, me_seq] = col_sent[g, me_seq]

    def attend_column(g):
        each(seq_count, lambda k: col_copy(g, k).wait_recv())
        result = attend(
            col_in[g].reshape(seq_count * seq_local, channels),
            seq_count * seq_local,
            col_entry,
            turned_value[1],
            col_gate[...],
            col_exit[...],
            mixed_col,
        )
        col_out[g] = result.astype(BF16).reshape(seq_count, seq_local, channels)
        each(seq_count, lambda k: col_return(g, k).start())
        col_back[g, me_seq] = col_out[g, me_seq]

    send_columns(0)
    attend_column(0)
    for h in range(1, halves):
        send_columns(h)
    for g in range(1, columns):
        attend_column(g)

    for i in (6, 7, 12, 13):
        loads[i].wait()
    for g in range(columns):
        each(seq_count, lambda k: col_return(g, k).wait_recv())
        tokens = seq_count * seq_local
        done = (
            after_turned[g].reshape(tokens, channels)
            + col_back[g].astype(F32).reshape(tokens, channels)
            + col_shift[...]
        )
        normed = standardize(done, gains[2:3], shifts[2:3])
        inner = jnp.maximum(dot(normed, ff_first[...]) + ff_first_shift[...], 0.0).astype(BF16)
        final = done + dot(inner, ff_second[...]) + ff_second_shift[...]
        for part in range(seq_count):
            out_ref[:, g * seq_count + part, :] = final[part * seq_local : (part + 1) * seq_local]

    for g in range(groups):
        each(res_count, lambda k: row_copy(g, k).wait_send())
        for h in range(halves):
            each(res_count, lambda k: row_return(h, g, k).wait_send())
    for g in range(columns):
        each(seq_count, lambda k: col_copy(g, k).wait_send())
        each(seq_count, lambda k: col_return(g, k).wait_send())


def shards(
    alignment_tensor,
    standardizer_factors,
    standardizer_offsets,
    horizontal_entry_matrix,
    horizontal_sigmoid_offset,
    horizontal_exit_matrix,
    horizontal_exit_offset,
    vertical_entry_matrix,
    vertical_sigmoid_offset,
    vertical_exit_matrix,
    vertical_exit_offset,
    feedforward_first_matrix,
    feedforward_first_offset,
    feedforward_second_matrix,
    feedforward_second_offset,
):
    seq_local, res_local, channels = alignment_tensor.shape
    hidden = feedforward_first_matrix.shape[1]
    res_count = lax.axis_size("res")
    seq_count = lax.axis_size("seq")
    items = seq_local // res_count
    group = 2 if items % 2 == 0 else 1
    groups = items // group
    columns = res_local // seq_count
    halves = 2 if columns % 2 == 0 and group % 2 == 0 and res_local % 16 == 0 else 1
    part_rows = res_local // halves
    vmem = pl.BlockSpec(memory_space=pltpu.VMEM)
    in_hbm = pl.BlockSpec(memory_space=pltpu.HBM)
    row_length, col_length = res_local * res_count, seq_local * seq_count

    def line(vector):
        return vector.reshape(1, -1)

    def mixed(length):
        rows = channels if length > 256 else 16
        wide = length if length > 256 else 128
        return [pltpu.VMEM((rows, wide), BF16), pltpu.VMEM((rows, wide), F32)]

    tokens = seq_local * res_local
    return pl.pallas_call(
        functools.partial(block, res_count, seq_count),
        out_shape=jax.ShapeDtypeStruct(alignment_tensor.shape, F32),
        in_specs=[in_hbm] * 15,
        out_specs=vmem,
        scratch_shapes=[
            pltpu.VMEM((res_count, groups, group, res_local, channels), F32),
            pltpu.VMEM(standardizer_factors.shape, F32),
            pltpu.VMEM(standardizer_offsets.shape, F32),
            pltpu.VMEM((1, channels), F32),
            pltpu.VMEM((1, channels), F32),
            pltpu.VMEM((1, channels), F32),
            pltpu.VMEM((1, channels), F32),
            pltpu.VMEM((1, hidden), F32),
            pltpu.VMEM((1, channels), F32),
            pltpu.VMEM(horizontal_entry_matrix.shape, BF16),
            pltpu.VMEM(horizontal_exit_matrix.shape, BF16),
            pltpu.VMEM(vertical_entry_matrix.shape, BF16),
            pltpu.VMEM(vertical_exit_matrix.shape, BF16),
            pltpu.VMEM(feedforward_first_matrix.shape, BF16),
            pltpu.VMEM(feedforward_second_matrix.shape, BF16),
            pltpu.VMEM((2, channels, channels), BF16),
            pltpu.VMEM((groups, res_count, group, res_local, channels), BF16),
            pltpu.VMEM((groups, res_count, group, res_local, channels), BF16),
            pltpu.VMEM((halves, groups, res_count, group * part_rows, channels), BF16),
            pltpu.VMEM((halves, res_count, groups, group * part_rows, channels), BF16),
            pltpu.VMEM((seq_local, res_local, channels), F32),
            pltpu.VMEM((columns, seq_count, seq_local, channels), F32),
            pltpu.VMEM((columns, seq_count, seq_local, channels), BF16),
            pltpu.VMEM((columns, seq_count, seq_local, channels), BF16),
            pltpu.VMEM((columns, seq_count, seq_local, channels), BF16),
            pltpu.VMEM((columns, seq_count, seq_local, channels), BF16),
            mixed(row_length),
            mixed(col_length),
            pltpu.SemaphoreType.DMA((groups,)),
            pltpu.SemaphoreType.DMA((14,)),
            pltpu.SemaphoreType.DMA((1, 2, groups, res_count)),
            pltpu.SemaphoreType.DMA((1, 2, halves * groups, res_count)),
            pltpu.SemaphoreType.DMA((2, 2, columns, seq_count)),
        ],
        compiler_params=pltpu.CompilerParams(
            collective_id=0, has_side_effects=True, vmem_limit_bytes=63 * 1024 * 1024
        ),
        cost_estimate=pl.CostEstimate(
            flops=2 * tokens * channels * (10 * channels + 2 * hidden),
            bytes_accessed=16 * tokens * channels,
            transcendentals=tokens * HEADS * (row_length + col_length),
        ),
    )(
        alignment_tensor.reshape(res_count, groups, group, res_local, channels),
        standardizer_factors,
        standardizer_offsets,
        line(horizontal_sigmoid_offset),
        line(horizontal_exit_offset),
        line(vertical_sigmoid_offset),
        line(vertical_exit_offset),
        line(feedforward_first_offset),
        line(feedforward_second_offset),
        horizontal_entry_matrix,
        horizontal_exit_matrix,
        vertical_entry_matrix,
        vertical_exit_matrix,
        feedforward_first_matrix,
        feedforward_second_matrix,
    )


def solution(mesh):
    return jax.shard_map(
        shards,
        mesh=mesh,
        in_specs=(P("seq", "res", None),) + (P(),) * 14,
        out_specs=P("seq", "res", None),
        check_vma=False,
    )
```

```python
import functools

import jax
import jax.numpy as jnp
from jax import lax
from jax.experimental import pallas as pl
from jax.experimental.pallas import tpu as pltpu
from jax.sharding import PartitionSpec as P

HEADS = 8
EPS = 1e-05
F32 = jnp.float32
BF16 = jnp.bfloat16
MESH = pl.DeviceIdType.MESH


def standardize(values, gain, shift):
    mean = jnp.mean(values, axis=-1, keepdims=True)
    centred = values - mean
    variance = jnp.mean(centred * centred, axis=-1, keepdims=True)
    return (centred * lax.rsqrt(variance + EPS) * gain + shift).astype(BF16)


def dot(left, right):
    return jnp.dot(left, right, preferred_element_type=F32)


def dot_nt(left, right):
    return lax.dot_general(left, right, (((1,), (1,)), ((), ())), preferred_element_type=F32)


def attend(normed, length, entry, value_turned, gate_offset, exit_matrix, mixed):
    channels = normed.shape[1]
    size = channels // HEADS
    count = normed.shape[0] // length
    query = (dot(normed, entry[:, :channels]) * size ** (-0.5)).astype(BF16)
    key = dot(normed, entry[:, channels : 2 * channels]).astype(BF16)
    gate = jax.nn.sigmoid(dot(normed, entry[:, 3 * channels :]) + gate_offset)
    spans = [slice(n * length, (n + 1) * length) for n in range(count)]
    value = dot_nt(value_turned, normed).astype(BF16)
    values = [value[:, span] for span in spans]
    ones = jnp.ones((16, length), BF16)
    lane = lax.broadcasted_iota(jnp.int32, (1, channels), 1)

    def weigh(score, value):
        weight = jnp.exp((score - jnp.max(score, axis=0, keepdims=True)).astype(BF16))
        return dot(jnp.concatenate([value, ones], axis=0), weight)

    def share(product):
        return product[:size] * (1.0 / product[size : size + 1])

    def mask(head):
        low = head * size
        return jnp.where((lane >= low) & (lane < low + size), 1.0, 0.0).astype(BF16)

    if length <= 256:
        masks = [mask(head) for head in range(HEADS)]
        scores = [
            dot_nt(jnp.concatenate([key[span] * m for m in masks], axis=0), query[span])
            for span in spans
        ]
        heads = [
            (value[h * size : (h + 1) * size], score[h * length : (h + 1) * length])
            for value, score in zip(values, scores)
            for h in range(HEADS)
        ]
        outs = [share(product) for product in [weigh(score, value) for value, score in heads]]
        turned = [
            jnp.concatenate(outs[n * HEADS : (n + 1) * HEADS], axis=0).T for n in range(count)
        ]
    else:
        held, out = mixed
        turned = []
        for span, value in zip(spans, values):
            held[...] = value

            def step(head, carry):
                rows = pl.ds(pl.multiple_of(head * size, size), size)
                score = dot_nt(key[span] * mask(head), query[span])
                out[rows, :] = share(weigh(score, held[rows, :]))
                return carry

            lax.fori_loop(0, HEADS, step, 0)
            turned.append(out[...].T)
    gated = (gate * jnp.concatenate(turned, axis=0)).astype(BF16)
    return dot(gated, exit_matrix)


def block(
    res_count,
    seq_count,
    x_hbm,
    gains_hbm,
    shifts_hbm,
    row_gate_hbm,
    row_shift_hbm,
    col_gate_hbm,
    col_shift_hbm,
    ff_first_shift_hbm,
    ff_second_shift_hbm,
    row_entry_hbm,
    row_exit_hbm,
    col_entry_hbm,
    col_exit_hbm,
    ff_first_hbm,
    ff_second_hbm,
    out_ref,
    x_ref,
    gains,
    shifts,
    row_gate,
    row_shift,
    col_gate,
    col_shift,
    ff_first_shift,
    ff_second_shift,
    row_entry,
    row_exit,
    col_entry,
    col_exit,
    ff_first,
    ff_second,
    turned_value,
    row_sent,
    row_in,
    row_out,
    row_back,
    after_row,
    after_turned,
    col_sent,
    col_in,
    col_out,
    col_back,
    mixed_row,
    mixed_col,
    x_sem,
    load_sem,
    send_sems,
    row_sems,
    back_sems,
    col_sems,
):
    me_res = lax.axis_index("res")
    me_seq = lax.axis_index("seq")
    groups, group = x_ref.shape[1], x_ref.shape[2]
    res_local, channels = x_ref.shape[3], x_ref.shape[4]
    seq_local = after_row.shape[0]
    items = groups * group
    row_length = res_count * res_local
    columns = res_local // seq_count
    halves = row_out.shape[0]
    part_rows, part_columns = res_local // halves, columns // halves

    barrier = pltpu.get_barrier_semaphore()

    def each(count, act):
        if count <= 8:
            for k in range(1, count):
                act(k)
        else:

            def step(k, carry):
                act(k)
                return carry

            lax.fori_loop(1, count, step, 0)

    def greet(axis, me, count):
        def act(k):
            peer = lax.rem(me + k, count)
            pl.semaphore_signal(barrier, inc=1, device_id={axis: peer}, device_id_type=MESH)

        each(count, act)

    greet("res", me_res, res_count)
    greet("seq", me_seq, seq_count)

    x_loads = [
        pltpu.make_async_copy(x_hbm.at[:, g], x_ref.at[:, g], x_sem.at[g]) for g in range(groups)
    ]
    pairs = (
        (gains_hbm, gains),
        (shifts_hbm, shifts),
        (row_gate_hbm, row_gate),
        (row_shift_hbm, row_shift),
        (col_gate_hbm, col_gate),
        (col_shift_hbm, col_shift),
        (ff_first_shift_hbm, ff_first_shift),
        (ff_second_shift_hbm, ff_second_shift),
        (row_entry_hbm, row_entry),
        (row_exit_hbm, row_exit),
        (col_entry_hbm, col_entry),
        (col_exit_hbm, col_exit),
        (ff_first_hbm, ff_first),
        (ff_second_hbm, ff_second),
    )
    loads = [
        pltpu.make_async_copy(src, dst, load_sem.at[i]) for i, (src, dst) in enumerate(pairs)
    ]
    for load in loads[:2] + x_loads + loads[2:]:
        load.start()

    def send(src, dst, axis, peer, phase, recv_sem):
        return pltpu.make_async_remote_copy(
            src_ref=src,
            dst_ref=dst,
            send_sem=send_sems.at[phase],
            recv_sem=recv_sem,
            device_id={axis: peer},
            device_id_type=MESH,
        )

    def row_copy(g, k):
        peer = lax.rem(me_res + k, res_count)
        return send(
            row_sent.at[g, peer], row_in.at[g, me_res], "res", peer, 0, row_sems.at[g]
        )

    def row_return(h, g, k):
        peer = lax.rem(me_res + k, res_count)
        return send(
            row_out.at[h, g, peer],
            row_back.at[h, g, me_res],
            "res",
            peer,
            1,
            back_sems.at[h * groups + g],
        )

    def col_copy(g, k):
        peer = lax.rem(me_seq + k, seq_count)
        return send(
            col_sent.at[g, peer], col_in.at[g, me_seq], "seq", peer, 2, col_sems.at[0, g]
        )

    def col_return(g, k):
        peer = lax.rem(me_seq + k, seq_count)
        return send(
            col_out.at[g, peer], col_back.at[g, me_seq], "seq", peer, 3, col_sems.at[1, g]
        )

    def arrived(buffer, sem):
        rest = buffer.at[pl.ds(0, buffer.shape[0] - 1)]
        pltpu.make_async_copy(rest, rest, sem).wait()

    def left(buffer, phase):
        rest = buffer.at[:, pl.ds(0, buffer.shape[1] - 1)]
        pltpu.make_async_copy(rest, rest, send_sems.at[phase]).wait()

    loads[0].wait()
    loads[1].wait()
    for g in range(groups):
        x_loads[g].wait()
        row_sent[g] = standardize(x_ref[:, g], gains[0:1], shifts[0:1])
        if g == 0:
            pl.semaphore_wait(barrier, res_count + seq_count - 2)
        each(res_count, lambda k: row_copy(g, k).start())
        row_in[g, me_res] = row_sent[g, me_res]

    for i in (2, 3, 8, 9):
        loads[i].wait()
    turned_value[0] = row_entry[:, 2 * channels : 3 * channels].T
    for g in range(groups):
        arrived(row_in.at[g], row_sems.at[g])
        result = attend(
            jnp.concatenate(
                [row_in[g, :, i].reshape(row_length, channels) for i in range(group)], axis=0
            ),
            row_length,
            row_entry,
            turned_value[0],
            row_gate[...],
            row_exit[...],
            mixed_row,
        )
        result = result.reshape(group, res_count, res_local, channels)
        for h in range(halves):
            rows = slice(h * part_rows, (h + 1) * part_rows)
            row_out[h, g] = jnp.concatenate(
                [result[i, :, rows] for i in range(group)], axis=1
            ).astype(BF16)
        each(res_count, lambda k: row_return(0, g, k).start())
        for h in range(1, halves):
            if g > 0:
                each(res_count, lambda k: row_return(h, g - 1, k).start())
            if g == groups - 1:
                each(res_count, lambda k: row_return(h, g, k).start())
        for h in range(halves):
            row_back[h, g, me_res] = row_out[h, g, me_res]

    for i in (4, 5, 10, 11):
        loads[i].wait()
    turned_value[1] = col_entry[:, 2 * channels : 3 * channels].T
    def send_columns(h):
        rows = slice(h * part_rows, (h + 1) * part_rows)
        for g in range(groups):
            arrived(row_back.at[h, g], back_sems.at[h * groups + g])
            for source in range(res_count):
                first = source * items + g * group
                back = row_back[h, g, source].astype(F32).reshape(group, part_rows, channels)
                after_row[first : first + group, rows] = (
                    x_ref[source, g, :, rows] + back + row_shift[...]
                )
        for g in range(h * part_columns, (h + 1) * part_columns):
            for part in range(seq_count):
                here = after_row[:, g * seq_count + part, :]
                after_turned[g, part] = here
                col_sent[g, part] = standardize(here, gains[1:2], shifts[1:2])
            each(seq_count, lambda k: col_copy(g, k).start())
            col_in[g, me_seq] = col_sent[g, me_seq]

    def attend_column(g):
        arrived(col_in.at[g], col_sems.at[0, g])
        result = attend(
            col_in[g].reshape(seq_count * seq_local, channels),
            seq_count * seq_local,
            col_entry,
            turned_value[1],
            col_gate[...],
            col_exit[...],
            mixed_col,
        )
        col_out[g] = result.astype(BF16).reshape(seq_count, seq_local, channels)
        each(seq_count, lambda k: col_return(g, k).start())
        col_back[g, me_seq] = col_out[g, me_seq]

    send_columns(0)
    attend_column(0)
    for h in range(1, halves):
        send_columns(h)
    for g in range(1, columns):
        attend_column(g)

    for i in (6, 7, 12, 13):
        loads[i].wait()
    for g in range(columns):
        arrived(col_back.at[g], col_sems.at[1, g])
        tokens = seq_count * seq_local
        done = (
            after_turned[g].reshape(tokens, channels)
            + col_back[g].astype(F32).reshape(tokens, channels)
            + col_shift[...]
        )
        normed = standardize(done, gains[2:3], shifts[2:3])
        inner = jnp.maximum(dot(normed, ff_first[...]) + ff_first_shift[...], 0.0).astype(BF16)
        final = done + dot(inner, ff_second[...]) + ff_second_shift[...]
        for part in range(seq_count):
            out_ref[:, g * seq_count + part, :] = final[part * seq_local : (part + 1) * seq_local]

    left(row_sent, 0)
    for h in range(halves):
        left(row_out.at[h], 1)
    left(col_sent, 2)
    left(col_out, 3)


def shards(
    alignment_tensor,
    standardizer_factors,
    standardizer_offsets,
    horizontal_entry_matrix,
    horizontal_sigmoid_offset,
    horizontal_exit_matrix,
    horizontal_exit_offset,
    vertical_entry_matrix,
    vertical_sigmoid_offset,
    vertical_exit_matrix,
    vertical_exit_offset,
    feedforward_first_matrix,
    feedforward_first_offset,
    feedforward_second_matrix,
    feedforward_second_offset,
):
    seq_local, res_local, channels = alignment_tensor.shape
    hidden = feedforward_first_matrix.shape[1]
    res_count = lax.axis_size("res")
    seq_count = lax.axis_size("seq")
    items = seq_local // res_count
    group = 2 if items % 2 == 0 else 1
    groups = items // group
    columns = res_local // seq_count
    halves = 1
    part_rows = res_local // halves
    vmem = pl.BlockSpec(memory_space=pltpu.VMEM)
    in_hbm = pl.BlockSpec(memory_space=pltpu.HBM)
    row_length, col_length = res_local * res_count, seq_local * seq_count

    def line(vector):
        return vector.reshape(1, -1)

    def mixed(length):
        rows = channels if length > 256 else 16
        wide = length if length > 256 else 128
        return [pltpu.VMEM((rows, wide), BF16), pltpu.VMEM((rows, wide), F32)]

    tokens = seq_local * res_local
    return pl.pallas_call(
        functools.partial(block, res_count, seq_count),
        out_shape=jax.ShapeDtypeStruct(alignment_tensor.shape, F32),
        in_specs=[in_hbm] * 15,
        out_specs=vmem,
        scratch_shapes=[
            pltpu.VMEM((res_count, groups, group, res_local, channels), F32),
            pltpu.VMEM(standardizer_factors.shape, F32),
            pltpu.VMEM(standardizer_offsets.shape, F32),
            pltpu.VMEM((1, channels), F32),
            pltpu.VMEM((1, channels), F32),
            pltpu.VMEM((1, channels), F32),
            pltpu.VMEM((1, channels), F32),
            pltpu.VMEM((1, hidden), F32),
            pltpu.VMEM((1, channels), F32),
            pltpu.VMEM(horizontal_entry_matrix.shape, BF16),
            pltpu.VMEM(horizontal_exit_matrix.shape, BF16),
            pltpu.VMEM(vertical_entry_matrix.shape, BF16),
            pltpu.VMEM(vertical_exit_matrix.shape, BF16),
            pltpu.VMEM(feedforward_first_matrix.shape, BF16),
            pltpu.VMEM(feedforward_second_matrix.shape, BF16),
            pltpu.VMEM((2, channels, channels), BF16),
            pltpu.VMEM((groups, res_count, group, res_local, channels), BF16),
            pltpu.VMEM((groups, res_count, group, res_local, channels), BF16),
            pltpu.VMEM((halves, groups, res_count, group * part_rows, channels), BF16),
            pltpu.VMEM((halves, groups, res_count, group * part_rows, channels), BF16),
            pltpu.VMEM((seq_local, res_local, channels), F32),
            pltpu.VMEM((columns, seq_count, seq_local, channels), F32),
            pltpu.VMEM((columns, seq_count, seq_local, channels), BF16),
            pltpu.VMEM((columns, seq_count, seq_local, channels), BF16),
            pltpu.VMEM((columns, seq_count, seq_local, channels), BF16),
            pltpu.VMEM((columns, seq_count, seq_local, channels), BF16),
            mixed(row_length),
            mixed(col_length),
            pltpu.SemaphoreType.DMA((groups,)),
            pltpu.SemaphoreType.DMA((14,)),
            pltpu.SemaphoreType.DMA((4,)),
            pltpu.SemaphoreType.DMA((groups,)),
            pltpu.SemaphoreType.DMA((halves * groups,)),
            pltpu.SemaphoreType.DMA((2, columns)),
        ],
        compiler_params=pltpu.CompilerParams(
            collective_id=0, has_side_effects=True, vmem_limit_bytes=63 * 1024 * 1024
        ),
        cost_estimate=pl.CostEstimate(
            flops=2 * tokens * channels * (10 * channels + 2 * hidden),
            bytes_accessed=16 * tokens * channels,
            transcendentals=tokens * HEADS * (row_length + col_length),
        ),
    )(
        alignment_tensor.reshape(res_count, groups, group, res_local, channels),
        standardizer_factors,
        standardizer_offsets,
        line(horizontal_sigmoid_offset),
        line(horizontal_exit_offset),
        line(vertical_sigmoid_offset),
        line(vertical_exit_offset),
        line(feedforward_first_offset),
        line(feedforward_second_offset),
        horizontal_entry_matrix,
        horizontal_exit_matrix,
        vertical_entry_matrix,
        vertical_exit_matrix,
        feedforward_first_matrix,
        feedforward_second_matrix,
    )


def solution(mesh):
    return jax.shard_map(
        shards,
        mesh=mesh,
        in_specs=(P("seq", "res", None),) + (P(),) * 14,
        out_specs=P("seq", "res", None),
        check_vma=False,
    )
```

```python
import functools

import jax
import jax.numpy as jnp
from jax import lax
from jax.experimental import pallas as pl
from jax.experimental.pallas import tpu as pltpu
from jax.sharding import PartitionSpec as P

HEADS = 8
EPS = 1e-05
F32 = jnp.float32
BF16 = jnp.bfloat16
MESH = pl.DeviceIdType.MESH


def standardize(values, gain, shift):
    mean = jnp.mean(values, axis=-1, keepdims=True)
    centred = values - mean
    variance = jnp.mean(centred * centred, axis=-1, keepdims=True)
    return (centred * lax.rsqrt(variance + EPS) * gain + shift).astype(BF16)


def dot(left, right):
    return jnp.dot(left, right, preferred_element_type=F32)


def dot_nt(left, right):
    return lax.dot_general(left, right, (((1,), (1,)), ((), ())), preferred_element_type=F32)


def attend(normed, length, entry, value_turned, gate_offset, exit_matrix, mixed):
    channels = normed.shape[1]
    size = channels // HEADS
    count = normed.shape[0] // length
    query = (dot(normed, entry[:, :channels]) * size ** (-0.5)).astype(BF16)
    key = dot(normed, entry[:, channels : 2 * channels]).astype(BF16)
    gate = jax.nn.sigmoid(dot(normed, entry[:, 3 * channels :]) + gate_offset)
    spans = [slice(n * length, (n + 1) * length) for n in range(count)]
    value = dot_nt(value_turned, normed).astype(BF16)
    values = [value[:, span] for span in spans]
    ones = jnp.ones((16, length), BF16)
    lane = lax.broadcasted_iota(jnp.int32, (1, channels), 1)

    def weigh(score, value):
        weight = jnp.exp((score - jnp.max(score, axis=0, keepdims=True)).astype(BF16))
        return dot(jnp.concatenate([value, ones], axis=0), weight)

    def share(product):
        return product[:size] * (1.0 / product[size : size + 1])

    def mask(head):
        low = head * size
        return jnp.where((lane >= low) & (lane < low + size), 1.0, 0.0).astype(BF16)

    if length <= 256:
        masks = [mask(head) for head in range(HEADS)]
        scores = [
            dot_nt(jnp.concatenate([key[span] * m for m in masks], axis=0), query[span])
            for span in spans
        ]
        heads = [
            (value[h * size : (h + 1) * size], score[h * length : (h + 1) * length])
            for value, score in zip(values, scores)
            for h in range(HEADS)
        ]
        outs = [share(product) for product in [weigh(score, value) for value, score in heads]]
        turned = [
            jnp.concatenate(outs[n * HEADS : (n + 1) * HEADS], axis=0).T for n in range(count)
        ]
    else:
        held, out = mixed
        turned = []
        for span, value in zip(spans, values):
            held[...] = value

            def step(head, carry):
                rows = pl.ds(pl.multiple_of(head * size, size), size)
                score = dot_nt(key[span] * mask(head), query[span])
                out[rows, :] = share(weigh(score, held[rows, :]))
                return carry

            lax.fori_loop(0, HEADS, step, 0)
            turned.append(out[...].T)
    gated = (gate * jnp.concatenate(turned, axis=0)).astype(BF16)
    return dot(gated, exit_matrix)


def block(
    res_count,
    seq_count,
    x_hbm,
    gains_hbm,
    shifts_hbm,
    row_gate_hbm,
    row_shift_hbm,
    col_gate_hbm,
    col_shift_hbm,
    ff_first_shift_hbm,
    ff_second_shift_hbm,
    row_entry_hbm,
    row_exit_hbm,
    col_entry_hbm,
    col_exit_hbm,
    ff_first_hbm,
    ff_second_hbm,
    out_ref,
    x_ref,
    gains,
    shifts,
    row_gate,
    row_shift,
    col_gate,
    col_shift,
    ff_first_shift,
    ff_second_shift,
    row_entry,
    row_exit,
    col_entry,
    col_exit,
    ff_first,
    ff_second,
    turned_value,
    row_sent,
    row_in,
    row_out,
    row_back,
    after_row,
    after_turned,
    col_sent,
    col_in,
    col_out,
    col_back,
    mixed_row,
    mixed_col,
    x_sem,
    load_sem,
    send_sems,
    row_sems,
    back_sems,
    col_sems,
):
    me_res = lax.axis_index("res")
    me_seq = lax.axis_index("seq")
    groups, group = x_ref.shape[1], x_ref.shape[2]
    res_local, channels = x_ref.shape[3], x_ref.shape[4]
    seq_local = after_row.shape[0]
    items = groups * group
    row_length = res_count * res_local
    columns = res_local // seq_count
    halves = row_out.shape[0]
    part_rows, part_columns = res_local // halves, columns // halves

    barrier = pltpu.get_barrier_semaphore()

    def each(count, act):
        if count <= 8:
            for k in range(1, count):
                act(k)
        else:

            def step(k, carry):
                act(k)
                return carry

            lax.fori_loop(1, count, step, 0)

    def greet(axis, me, count):
        def act(k):
            peer = lax.rem(me + k, count)
            pl.semaphore_signal(barrier, inc=1, device_id={axis: peer}, device_id_type=MESH)

        each(count, act)

    greet("res", me_res, res_count)
    greet("seq", me_seq, seq_count)

    x_loads = [
        pltpu.make_async_copy(x_hbm.at[:, g], x_ref.at[:, g], x_sem.at[g]) for g in range(groups)
    ]
    pairs = (
        (gains_hbm, gains),
        (shifts_hbm, shifts),
        (row_gate_hbm, row_gate),
        (row_shift_hbm, row_shift),
        (col_gate_hbm, col_gate),
        (col_shift_hbm, col_shift),
        (ff_first_shift_hbm, ff_first_shift),
        (ff_second_shift_hbm, ff_second_shift),
        (row_entry_hbm, row_entry),
        (row_exit_hbm, row_exit),
        (col_entry_hbm, col_entry),
        (col_exit_hbm, col_exit),
        (ff_first_hbm, ff_first),
        (ff_second_hbm, ff_second),
    )
    loads = [
        pltpu.make_async_copy(src, dst, load_sem.at[i]) for i, (src, dst) in enumerate(pairs)
    ]
    for load in loads[:2] + x_loads + loads[2:]:
        load.start()

    def send(src, dst, axis, peer, phase, recv_sem):
        return pltpu.make_async_remote_copy(
            src_ref=src,
            dst_ref=dst,
            send_sem=send_sems.at[phase],
            recv_sem=recv_sem,
            device_id={axis: peer},
            device_id_type=MESH,
        )

    def row_copy(g, k):
        peer = lax.rem(me_res + k, res_count)
        return send(
            row_sent.at[g, peer], row_in.at[g, me_res], "res", peer, 0, row_sems.at[g]
        )

    def row_return(h, g, k):
        peer = lax.rem(me_res + k, res_count)
        return send(
            row_out.at[h, g, peer],
            row_back.at[h, g, me_res],
            "res",
            peer,
            1,
            back_sems.at[h * groups + g],
        )

    def col_copy(g, k):
        peer = lax.rem(me_seq + k, seq_count)
        return send(
            col_sent.at[g, peer], col_in.at[g, me_seq], "seq", peer, 2, col_sems.at[0, g]
        )

    def col_return(g, k):
        peer = lax.rem(me_seq + k, seq_count)
        return send(
            col_out.at[g, peer], col_back.at[g, me_seq], "seq", peer, 3, col_sems.at[1, g]
        )

    def arrived(buffer, sem):
        rest = buffer.at[pl.ds(0, buffer.shape[0] - 1)]
        pltpu.make_async_copy(rest, rest, sem).wait()

    def left(buffer, phase):
        rest = buffer.at[:, pl.ds(0, buffer.shape[1] - 1)]
        pltpu.make_async_copy(rest, rest, send_sems.at[phase]).wait()

    loads[0].wait()
    loads[1].wait()
    for g in range(groups):
        x_loads[g].wait()
        row_sent[g] = standardize(x_ref[:, g], gains[0:1], shifts[0:1])
        if g == 0:
            pl.semaphore_wait(barrier, res_count + seq_count - 2)
        each(res_count, lambda k: row_copy(g, k).start())
        row_in[g, me_res] = row_sent[g, me_res]

    for i in (2, 3, 8, 9):
        loads[i].wait()
    turned_value[0] = row_entry[:, 2 * channels : 3 * channels].T
    for g in range(groups):
        arrived(row_in.at[g], row_sems.at[g])
        result = attend(
            jnp.concatenate(
                [row_in[g, :, i].reshape(row_length, channels) for i in range(group)], axis=0
            ),
            row_length,
            row_entry,
            turned_value[0],
            row_gate[...],
            row_exit[...],
            mixed_row,
        )
        result = result.reshape(group, res_count, res_local, channels)
        for h in range(halves):
            rows = slice(h * part_rows, (h + 1) * part_rows)
            row_out[h, g] = jnp.concatenate(
                [result[i, :, rows] for i in range(group)], axis=1
            ).astype(BF16)
        each(res_count, lambda k: row_return(0, g, k).start())
        for h in range(1, halves):
            if g > 0:
                each(res_count, lambda k: row_return(h, g - 1, k).start())
            if g == groups - 1:
                each(res_count, lambda k: row_return(h, g, k).start())
        for h in range(halves):
            row_back[h, g, me_res] = row_out[h, g, me_res]

    for i in (4, 5, 10, 11):
        loads[i].wait()
    turned_value[1] = col_entry[:, 2 * channels : 3 * channels].T
    def send_columns(h):
        rows = slice(h * part_rows, (h + 1) * part_rows)
        for g in range(groups):
            arrived(row_back.at[h, g], back_sems.at[h * groups + g])
            for source in range(res_count):
                first = source * items + g * group
                back = row_back[h, g, source].astype(F32).reshape(group, part_rows, channels)
                after_row[first : first + group, rows] = (
                    x_ref[source, g, :, rows] + back + row_shift[...]
                )
        for g in range(h * part_columns, (h + 1) * part_columns):
            for part in range(seq_count):
                here = after_row[:, g * seq_count + part, :]
                after_turned[g, part] = here
                col_sent[g, part] = standardize(here, gains[1:2], shifts[1:2])
            each(seq_count, lambda k: col_copy(g, k).start())
            col_in[g, me_seq] = col_sent[g, me_seq]

    def attend_column(g):
        arrived(col_in.at[g], col_sems.at[0, g])
        result = attend(
            col_in[g].reshape(seq_count * seq_local, channels),
            seq_count * seq_local,
            col_entry,
            turned_value[1],
            col_gate[...],
            col_exit[...],
            mixed_col,
        )
        col_out[g] = result.astype(BF16).reshape(seq_count, seq_local, channels)
        each(seq_count, lambda k: col_return(g, k).start())
        col_back[g, me_seq] = col_out[g, me_seq]

    send_columns(0)
    attend_column(0)
    for h in range(1, halves):
        send_columns(h)
    for g in range(1, columns):
        attend_column(g)

    for i in (6, 7, 12, 13):
        loads[i].wait()
    for g in range(columns):
        arrived(col_back.at[g], col_sems.at[1, g])
        tokens = seq_count * seq_local
        done = (
            after_turned[g].reshape(tokens, channels)
            + col_back[g].astype(F32).reshape(tokens, channels)
            + col_shift[...]
        )
        normed = standardize(done, gains[2:3], shifts[2:3])
        inner = jnp.maximum(dot(normed, ff_first[...]) + ff_first_shift[...], 0.0).astype(BF16)
        final = done + dot(inner, ff_second[...]) + ff_second_shift[...]
        for part in range(seq_count):
            after_row[:, g * seq_count + part, :] = final[part * seq_local : (part + 1) * seq_local]

    out_ref[...] = after_row[...].astype(BF16)

    left(row_sent, 0)
    for h in range(halves):
        left(row_out.at[h], 1)
    left(col_sent, 2)
    left(col_out, 3)


def shards(
    alignment_tensor,
    standardizer_factors,
    standardizer_offsets,
    horizontal_entry_matrix,
    horizontal_sigmoid_offset,
    horizontal_exit_matrix,
    horizontal_exit_offset,
    vertical_entry_matrix,
    vertical_sigmoid_offset,
    vertical_exit_matrix,
    vertical_exit_offset,
    feedforward_first_matrix,
    feedforward_first_offset,
    feedforward_second_matrix,
    feedforward_second_offset,
):
    seq_local, res_local, channels = alignment_tensor.shape
    hidden = feedforward_first_matrix.shape[1]
    res_count = lax.axis_size("res")
    seq_count = lax.axis_size("seq")
    items = seq_local // res_count
    group = 2 if items % 2 == 0 else 1
    groups = items // group
    columns = res_local // seq_count
    halves = 1
    part_rows = res_local // halves
    vmem = pl.BlockSpec(memory_space=pltpu.VMEM)
    in_hbm = pl.BlockSpec(memory_space=pltpu.HBM)
    row_length, col_length = res_local * res_count, seq_local * seq_count

    def line(vector):
        return vector.reshape(1, -1)

    def mixed(length):
        rows = channels if length > 256 else 16
        wide = length if length > 256 else 128
        return [pltpu.VMEM((rows, wide), BF16), pltpu.VMEM((rows, wide), F32)]

    tokens = seq_local * res_local
    return pl.pallas_call(
        functools.partial(block, res_count, seq_count),
        out_shape=jax.ShapeDtypeStruct(alignment_tensor.shape, BF16),
        in_specs=[in_hbm] * 15,
        out_specs=vmem,
        scratch_shapes=[
            pltpu.VMEM((res_count, groups, group, res_local, channels), F32),
            pltpu.VMEM(standardizer_factors.shape, F32),
            pltpu.VMEM(standardizer_offsets.shape, F32),
            pltpu.VMEM((1, channels), F32),
            pltpu.VMEM((1, channels), F32),
            pltpu.VMEM((1, channels), F32),
            pltpu.VMEM((1, channels), F32),
            pltpu.VMEM((1, hidden), F32),
            pltpu.VMEM((1, channels), F32),
            pltpu.VMEM(horizontal_entry_matrix.shape, BF16),
            pltpu.VMEM(horizontal_exit_matrix.shape, BF16),
            pltpu.VMEM(vertical_entry_matrix.shape, BF16),
            pltpu.VMEM(vertical_exit_matrix.shape, BF16),
            pltpu.VMEM(feedforward_first_matrix.shape, BF16),
            pltpu.VMEM(feedforward_second_matrix.shape, BF16),
            pltpu.VMEM((2, channels, channels), BF16),
            pltpu.VMEM((groups, res_count, group, res_local, channels), BF16),
            pltpu.VMEM((groups, res_count, group, res_local, channels), BF16),
            pltpu.VMEM((halves, groups, res_count, group * part_rows, channels), BF16),
            pltpu.VMEM((halves, groups, res_count, group * part_rows, channels), BF16),
            pltpu.VMEM((seq_local, res_local, channels), F32),
            pltpu.VMEM((columns, seq_count, seq_local, channels), F32),
            pltpu.VMEM((columns, seq_count, seq_local, channels), BF16),
            pltpu.VMEM((columns, seq_count, seq_local, channels), BF16),
            pltpu.VMEM((columns, seq_count, seq_local, channels), BF16),
            pltpu.VMEM((columns, seq_count, seq_local, channels), BF16),
            mixed(row_length),
            mixed(col_length),
            pltpu.SemaphoreType.DMA((groups,)),
            pltpu.SemaphoreType.DMA((14,)),
            pltpu.SemaphoreType.DMA((4,)),
            pltpu.SemaphoreType.DMA((groups,)),
            pltpu.SemaphoreType.DMA((halves * groups,)),
            pltpu.SemaphoreType.DMA((2, columns)),
        ],
        compiler_params=pltpu.CompilerParams(
            collective_id=0, has_side_effects=True, vmem_limit_bytes=63 * 1024 * 1024
        ),
        cost_estimate=pl.CostEstimate(
            flops=2 * tokens * channels * (10 * channels + 2 * hidden),
            bytes_accessed=16 * tokens * channels,
            transcendentals=tokens * HEADS * (row_length + col_length),
        ),
    )(
        alignment_tensor.reshape(res_count, groups, group, res_local, channels),
        standardizer_factors,
        standardizer_offsets,
        line(horizontal_sigmoid_offset),
        line(horizontal_exit_offset),
        line(vertical_sigmoid_offset),
        line(vertical_exit_offset),
        line(feedforward_first_offset),
        line(feedforward_second_offset),
        horizontal_entry_matrix,
        horizontal_exit_matrix,
        vertical_entry_matrix,
        vertical_exit_matrix,
        feedforward_first_matrix,
        feedforward_second_matrix,
    ).astype(F32)


def solution(mesh):
    return jax.shard_map(
        shards,
        mesh=mesh,
        in_specs=(P("seq", "res", None),) + (P(),) * 14,
        out_specs=P("seq", "res", None),
        check_vma=False,
    )
```
